128 devices in a mesh: role: 2 (over y_lo), grp: 64 (over y_hi, z, x, core).
Axes of the slice: x: 4, y: 4 (y_hi: 2, y_lo: 2; y = y_hi * 2 + y_lo), z: 4, core: 2. Of those that a mesh axis runs over, the one named last changes fastest.
Arguments:
- hidden_state: float32 [128, 8192], P(None, ('role', 'grp')), may hold values from -6 to 6
- gain_attn: float32 [8192], P(('role', 'grp')), may hold values from 0.25 to 1.75
- gain_ffn: float32 [8192], P(('role', 'grp')), may hold values from 0.25 to 1.75
- w_qkv: bfloat16 [9216, 8192], P(('role', 'grp')), may hold values from -0.0625 to 0.0625
- w_out: bfloat16 [8192, 8192], P(('role', 'grp')), may hold values from -0.0625 to 0.0625
- w_gate: bfloat16 [53248, 8192], P(('role', 'grp')), may hold values from -0.0625 to 0.0625
- w_up: bfloat16 [53248, 8192], P(('role', 'grp')), may hold values from -0.0625 to 0.0625
- w_down: bfloat16 [53248, 8192], P(('role', 'grp')), may hold values from -0.02734375 to 0.02734375
- kv_cache: bfloat16 [128, 1024, 1024], P(('role', 'grp'))
- lengths: int32 [128], replicated, may hold values from 1 to 1024, as said below
- row_order: int32 [128], replicated, may hold values from 0 to 127, each once
Outputs:
- out_state: float32 [128, 8192], P(None, ('role', 'grp'))
The draws below stay inside these ranges and needn't reach their ends.
Inputs may be any that keep to these rules, and one draw needn't show every extreme that they name: `lengths`: every sequence has at least one cached position; some sequence has all 1024. `row_order`: each sequence is named by exactly one cache row.
All inputs are finite; a program needn't handle non-finite values.
Results may differ from the reference program's by a relative error of at most 0.0099.
Values may be sent and summed in bfloat16 or wider, within the bound.
A program may use at most 128 MiB of HBM per device.

```python
import jax
import jax.numpy as jnp
from jax import lax

D = 8192
QH = 64
KVH = 4
HD = 128
FF = 53248
STEPS = 1
ROWS = 128
CACHE = 1024


def draw_kv_cache(key, part):
    key = jax.random.fold_in(key, 11)
    first = jax.random.fold_in(key, 0)
    base = jax.random.normal(first, (ROWS, CACHE, 2 * KVH * HD), jnp.float32)
    return base.astype(jnp.bfloat16)


def draw_lengths(key, part):
    key = jax.random.fold_in(key, 23)
    first, second = jax.random.split(key)
    counts = jax.random.randint(first, (ROWS,), 1, CACHE + 1, jnp.int32)
    where_full = jax.random.randint(second, (), 0, ROWS, jnp.int32)
    return counts.at[where_full].set(CACHE)


def steps_of(stream_key, shape, cuts, low, high):
    level, own = 1.0, jax.random.fold_in(stream_key, 6)
    for position, parts in cuts:
        heights = jnp.exp(jax.random.uniform(jax.random.fold_in(own, position), (parts,), jnp.float32, low / len(cuts), high / len(cuts)))
        level = level * jnp.repeat(heights, shape[position] // parts).reshape([-1 if axis == position else 1 for axis in range(len(shape))])
    return level


def centred(own_key, dims, scale, limit, pieces=(), kind=jnp.bfloat16):
    drawn = scale * jax.random.normal(own_key, dims, jnp.float32)
    if pieces:
        drawn = drawn * steps_of(own_key, dims, pieces, -0.22, 0.18)
    return jnp.clip(drawn, -limit, limit).astype(kind)


def setup_inputs(seed: int = 0) -> dict:
    key_list = jax.random.split(jax.random.key(seed), 12)
    hidden_state = centred(key_list[0], (ROWS, D), 1.0, 6.0, ((1, 128),), jnp.float32)
    gain_attn = jnp.clip(1.0 + 0.15 * jax.random.normal(key_list[1], (D,), jnp.float32), 0.25, 1.75)
    gain_ffn = jnp.clip(1.0 + 0.15 * jax.random.normal(key_list[2], (D,), jnp.float32), 0.25, 1.75)
    w_qkv = centred(key_list[3], ((QH + 2 * KVH) * HD, D), D ** -0.5, 0.0625, ((0, 128),))
    w_out = centred(key_list[4], (D, QH * HD), (QH * HD) ** -0.5, 0.0625, ((0, 128),))
    w_gate = centred(key_list[5], (FF, D), D ** -0.5, 0.0625, ((0, 128),))
    w_up = centred(key_list[6], (FF, D), D ** -0.5, 0.0625, ((0, 128),))
    w_down = centred(key_list[7], (FF, D), FF ** -0.5, 0.02734375, ((0, 128),))
    kv_cache = draw_kv_cache(jax.random.fold_in(key_list[11], 71), 0)
    lengths = draw_lengths(jax.random.fold_in(key_list[11], 71), 0)
    row_order = jax.random.permutation(key_list[10], ROWS).astype(jnp.int32)
    return dict(hidden_state=hidden_state, gain_attn=gain_attn, gain_ffn=gain_ffn, w_qkv=w_qkv, w_out=w_out, w_gate=w_gate, w_up=w_up, w_down=w_down, kv_cache=kv_cache, lengths=lengths, row_order=row_order)


def rms_normed(values, gain):
    mean = lax.optimization_barrier(jnp.mean(values * values, axis=1, keepdims=True))
    return (values * lax.rsqrt(mean + 1e-05) * gain).astype(jnp.bfloat16)

def attend_rows(operands):
    query, cache, lens, fresh_all = operands
    rows = query.shape[0]
    length = cache.shape[1]
    count = fresh_all.shape[1]
    key_width = KVH * HD
    groups = QH // KVH
    scale = 1.0 / HD ** 0.5
    query = query.astype(jnp.float32).reshape(rows, KVH, groups, HD)
    keys = cache[:, :, :key_width].astype(jnp.float32).reshape(rows, length, KVH, HD)
    values = cache[:, :, key_width:].astype(jnp.float32).reshape(rows, length, KVH, HD)
    new_keys = fresh_all[:, :, :key_width].astype(jnp.float32).reshape(rows, count, KVH, HD)
    new_values = fresh_all[:, :, key_width:].astype(jnp.float32).reshape(rows, count, KVH, HD)
    valid = (jnp.arange(length, dtype=jnp.int32)[None, :] < lens[:, None])[:, None, None, :]
    cached = jnp.einsum('rkgd,rlkd->rkgl', query, keys) * scale
    cached = jnp.where(valid, cached, -1e+30)
    fresh = jnp.einsum('rkgd,rjkd->rkgj', query, new_keys) * scale
    top = jnp.maximum(lax.optimization_barrier(jnp.max(cached, axis=-1)), lax.optimization_barrier(jnp.max(fresh, axis=-1)))
    cached_w = jnp.where(valid, jnp.exp(cached - top[..., None]), 0.0)
    fresh_w = jnp.exp(fresh - top[..., None])
    total = lax.optimization_barrier(jnp.sum(cached_w, axis=-1)) + lax.optimization_barrier(jnp.sum(fresh_w, axis=-1))
    cached_b = lax.optimization_barrier(cached_w.astype(jnp.bfloat16)).astype(jnp.float32)
    fresh_b = lax.optimization_barrier(fresh_w.astype(jnp.bfloat16)).astype(jnp.float32)
    summed = jnp.einsum('rkgl,rlkd->rkgd', cached_b, values) + jnp.einsum('rkgj,rjkd->rkgd', fresh_b, new_values)
    return (summed / total[..., None]).reshape(rows, QH * HD).astype(jnp.bfloat16)

def reference(hidden_state, gain_attn, gain_ffn, w_qkv, w_out, w_gate, w_up, w_down, kv_cache, lengths, row_order):
    query_width = QH * HD
    inverse = jnp.argsort(row_order).astype(jnp.int32)
    state = hidden_state[row_order]
    lens = lengths[row_order]
    blocks = ROWS // 16
    recent = []
    for step in range(STEPS):
        normed_a = rms_normed(state, gain_attn)
        projected = jnp.dot(normed_a, w_qkv.T, preferred_element_type=jnp.float32).astype(jnp.bfloat16)
        query = projected[:, :query_width]
        recent.append(projected[:, query_width:])
        fresh_all = jnp.stack(recent, axis=1)
        attended = lax.map(attend_rows, (query.reshape(blocks, 16, query_width), kv_cache.reshape(blocks, 16, CACHE, 2 * KVH * HD), lens.reshape(blocks, 16), fresh_all.reshape(blocks, 16, len(recent), 2 * KVH * HD)))
        attended = attended.reshape(ROWS, query_width)
        state = state + jnp.dot(attended, w_out.T, preferred_element_type=jnp.float32)
        normed_f = rms_normed(state, gain_ffn)
        gate = jnp.dot(normed_f, w_gate.T, preferred_element_type=jnp.float32)
        upper = jnp.dot(normed_f, w_up.T, preferred_element_type=jnp.float32)
        hidden = (jax.nn.silu(gate) * upper).astype(jnp.bfloat16)
        state = state + jnp.dot(hidden, w_down, preferred_element_type=jnp.float32)
    return state[inverse]
```

```python
import jax
import jax.numpy as jnp
from jax import lax
from jax.experimental import pallas as pl
from jax.experimental.pallas import tpu as pltpu
from jax.sharding import PartitionSpec as P

F32 = jnp.float32
BF16 = jnp.bfloat16
D = 8192
QH = 64
KVH = 4
HD = 128
ROWS = 128
DEVICES = 128
FEATURES = D // DEVICES
QKV = (QH + 2 * KVH) * HD // DEVICES
FF = 53248 // DEVICES
CACHE = 1024
EPS = 1e-05
AXES = "yzx"
MESH = pl.DeviceIdType.MESH

PARTS = ((0, 16, "xzy"), (16, 16, "zyx"), (32, 32, "yxz"))
GATHER_SEMS = 13


def iota(shape, dim):
    return lax.broadcasted_iota(jnp.int32, shape, dim)


def dot(a, b, ca=1, cb=0):
    return lax.dot_general(a, b, (((ca,), (cb,)), ((), ())), preferred_element_type=F32)


def kernel(
    hs_ref, ga_ref, gf_ref, len_ref, ord_ref,
    wqkv_hbm, wout_hbm, wg_hbm, wu_hbm, wd_hbm, kv_hbm,
    out_ref,
    wqkv, wout, wg, wu, wd, kv, load_sem,
    xa, sa, xf, sf, a1, fold, att, t_buf, r1, r2,
    pt, rc, rb0, rb1, rb2, fs,
    hid_ref, gate_ref, up_ref,
    xa_send, xa_recv, sa_send, sa_recv, xf_send, xf_recv, sf_send, sf_recv,
    at_send, at_recv, aa_send, aa_recv, rs_send, rs_recv,
):
    role = lax.axis_index("role")
    grp = lax.axis_index("grp")
    c = lax.rem(grp, 2)
    coord = {
        "x": lax.rem(lax.div(grp, 2), 4),
        "z": lax.rem(lax.div(grp, 8), 4),
        "y": role * 2 + lax.div(grp, 32),
    }
    me = role * 64 + grp

    def device(at, core):
        y = at["y"]
        return (lax.div(y, 2), lax.rem(y, 2) * 32 + at["z"] * 8 + at["x"] * 2 + core)

    def shifted(axis, k):
        return {**coord, axis: lax.rem(coord[axis] + k + 4, 4)}

    def peer(axis, k):
        return device(shifted(axis, k), c)

    sibling = device(coord, 1 - c)

    def index(at, full):
        return tuple(slice(None) if a in full else at[a] for a in AXES)

    pending = []

    def send(src, dst, send_sem, recv_sem, target):
        copy = pltpu.make_async_remote_copy(
            src_ref=src, dst_ref=dst, send_sem=send_sem, recv_sem=recv_sem,
            device_id=target, device_id_type=MESH,
        )
        copy.start()
        pending.append(copy)
        return copy

    loads = []
    for i, (src, dst) in enumerate(
        ((wqkv_hbm, wqkv), (kv_hbm, kv), (wout_hbm, wout), (wg_hbm, wg), (wu_hbm, wu), (wd_hbm, wd))
    ):
        load = pltpu.make_async_copy(src, dst, load_sem.at[i])
        load.start()
        loads.append(load)

    others = [sibling]
    for axis in AXES:
        others += [peer(axis, k) for k in (1, 2, 3)]
    for k in (1, 2, 3):
        others.append(device(shifted("x", k), 1 - c))
    for ky in (1, 2, 3):
        for kz in (1, 2, 3):
            others.append(device({**shifted("z", kz), "y": shifted("y", ky)["y"]}, c))
    barrier = pltpu.get_barrier_semaphore()
    for other in others:
        pl.semaphore_signal(barrier, inc=1, device_id=other, device_id_type=MESH)

    def transposed(v):
        return jnp.concatenate([v, jnp.zeros_like(v)], axis=1).T[:FEATURES]

    state = transposed(hs_ref[...])
    gain_f = transposed(jnp.broadcast_to(gf_ref[...], (ROWS, FEATURES)))
    gain_a = transposed(jnp.broadcast_to(ga_ref[...], (ROWS, FEATURES)))
    own = tuple(coord[a] for a in AXES)
    xa[own + (c,)] = (state * gain_a).astype(BF16)
    sa[own + (c,)] = jnp.sum(state * state, axis=0, keepdims=True)

    order_row = ord_ref[...]
    by_seq = (iota((ROWS, ROWS), 0) == order_row).astype(F32)
    by_slot = by_seq.T.astype(BF16)
    lane = iota((1, ROWS), 1)
    my_seq = jnp.sum(jnp.where(lane == me, order_row, 0), axis=1, keepdims=True)
    my_len = jnp.sum(jnp.where(lane == my_seq, len_ref[...], 0), axis=1, keepdims=True)

    pl.semaphore_wait(barrier, len(others))

    class Gather:
        def __init__(self, buf, order, tail, send_sem, recv_sem, base, cored=True):
            self.buf, self.order, self.tail = buf, order, tail
            self.send_sem, self.recv_sem, self.base = send_sem, recv_sem, base
            self.copies = [[], [], [], []]

        def go(self, stage, sem, where, target):
            ref = self.buf.at[where + (c,) + self.tail]
            sem = self.base + sem
            self.copies[stage].append(
                send(ref, ref, self.send_sem.at[sem], self.recv_sem.at[sem], target)
            )

        def step(self, stage):
            if stage:
                for copy in self.copies[stage - 1]:
                    copy.wait_recv()
            where = index(coord, self.order[:stage])
            for k in (2, 1, 3):
                self.go(stage, stage * 3 + k - 1, where, peer(self.order[stage], k))
            if stage == 2:
                self.go(3, 9, where, sibling)

        def last(self, k):
            self.copies[2][(2, 1, 3).index(k)].wait_recv()
            where = index(shifted(self.order[2], -k), self.order[:2])
            self.go(3, 9 + k, where, sibling)

        def finish(self):
            for copy in self.copies[3]:
                copy.wait_recv()

    def run_gather(gathers):
        for stage in range(3):
            for g in gathers:
                g.step(stage)
        for k in (1, 3, 2):
            for g in gathers:
                g.last(k)
        for g in gathers:
            g.finish()

    def state_gather(x, s, x_send, x_recv, s_send, s_recv):
        gathers = [Gather(s, "xzy", (), s_send, s_recv, 0)]
        for p, (at, n, order) in enumerate(PARTS):
            gathers.append(Gather(x, order, (pl.ds(at, n),), x_send, x_recv, p * GATHER_SEMS))
        run_gather(gathers)

    def row_scale(s):
        total = jnp.sum(s[...].reshape(DEVICES, ROWS), axis=0, keepdims=True)
        return lax.rsqrt(total * (1.0 / D) + EPS)

    state_gather(xa, sa, xa_send, xa_recv, sa_send, sa_recv)
    loads[0].wait()
    proj = jnp.zeros((QKV, ROWS), F32)
    for y in range(4):
        block = xa[y].reshape(D // 4, ROWS)
        proj = proj + dot(wqkv[:, y * (D // 4):(y + 1) * (D // 4)], block)
    proj = (proj * row_scale(sa)).astype(BF16)

    lane_of = lax.rem(me * QKV + iota((QKV, HD), 0), HD)
    place = (lane_of == iota((QKV, HD), 1)).astype(BF16)
    placed = dot(proj, place, 0, 0).astype(BF16)
    t_buf[...] = dot(by_slot, placed).reshape(16, 8, 1, HD)
    xc = coord["x"] * 2 + c
    yz = coord["y"] * 4 + coord["z"]
    first, second = [], []
    n = 0
    for kx in range(4):
        for kc in range(2):
            if kx or kc:
                at, core = shifted("x", kx), lax.rem(c + kc, 2)
                first.append(send(t_buf.at[:, at["x"] * 2 + core], r1.at[xc],
                                  aa_send.at[n], aa_recv.at[n], device(at, core)))
                n += 1
    r1[xc] = t_buf[:, xc]
    for copy in first:
        copy.wait_recv()
    for ky in range(4):
        for kz in range(4):
            if ky or kz:
                at = {**shifted("z", kz), "y": shifted("y", ky)["y"]}
                second.append(send(r1.at[:, at["y"] * 4 + at["z"]], r2.at[yz],
                                   aa_send.at[n], aa_recv.at[n], device(at, c)))
                n += 1
    r2[yz] = r1[:, yz]
    for copy in second:
        copy.wait_recv()
    got = r2[...].reshape(DEVICES, HD)
    start = iota((DEVICES, HD), 0) * QKV
    late = iota((DEVICES, HD), 1) >= lax.rem(start, HD)
    heads = QH + 2 * KVH
    src_head = lax.div(iota((heads, DEVICES), 1) * QKV, HD)
    head = iota((heads, DEVICES), 0)
    qkv = dot((src_head == head).astype(BF16), jnp.where(late, got, 0.0).astype(BF16))
    qkv = qkv + dot((src_head + 1 == head).astype(BF16), jnp.where(late, 0.0, got).astype(BF16))

    loads[1].wait()
    groups = QH // KVH
    valid = iota((groups, CACHE), 1) < my_len
    outs = []
    for h in range(KVH):
        q = qkv[h * groups:(h + 1) * groups]
        k_new = qkv[QH + h:QH + h + 1]
        v_new = qkv[QH + KVH + h:QH + KVH + h + 1]
        keys = kv[0, :, h * HD:(h + 1) * HD]
        values = kv[0, :, (KVH + h) * HD:(KVH + h + 1) * HD]
        cached = jnp.where(valid, dot(q.astype(BF16), keys, 1, 1) * (1.0 / HD ** 0.5), -1e30)
        fresh = jnp.sum(q * k_new, axis=1, keepdims=True) * (1.0 / HD ** 0.5)
        top = jnp.maximum(jnp.max(cached, axis=1, keepdims=True), fresh)
        cached_w = jnp.where(valid, jnp.exp(cached - top), 0.0)
        fresh_w = jnp.exp(fresh - top)
        total = jnp.sum(cached_w, axis=1, keepdims=True) + fresh_w
        summed = dot(cached_w.astype(BF16), values) + fresh_w.astype(BF16).astype(F32) * v_new
        outs.append((summed / total).astype(BF16))
    a1[own] = jnp.concatenate(outs, axis=0)

    def plane_step(p, stage, done):
        at, n, order = PARTS[p]
        for copy in done:
            copy.wait_recv()
        ref = a1.at[index(coord, order[:stage]) + (pl.ds(at, n),)]
        sems = [p * GATHER_SEMS + stage * 3 + k - 1 for k in (1, 2, 3)]
        return [send(ref, ref, at_send.at[s], at_recv.at[s], peer(order[stage], k))
                for k, s in zip((1, 2, 3), sems)]

    def att_ref(p, where):
        at, n, order = PARTS[p]
        return att.at[pl.ds(at, n), where[order[2]] * 2 + c]

    stages = [[] for _ in PARTS]
    for stage in range(2):
        for p in range(len(PARTS)):
            stages[p] = plane_step(p, stage, stages[p])
    to_sibling = [[] for _ in PARTS]
    for p, (at, n, order) in enumerate(PARTS):
        for copy in stages[p]:
            copy.wait_recv()
        plane = a1[index(coord, order[:2]) + (slice(at, at + n),)].reshape(16 * n, HD)
        fold[0:16 * n] = plane.astype(F32)
        rows = [fold[pl.ds(h, 16, stride=n)] for h in range(n)]
        att[pl.ds(at, n), coord[order[2]] * 2 + c] = jnp.stack(rows).astype(BF16)
        stages[p] = []
        for k in (1, 2, 3):
            s = p * GATHER_SEMS + 6 + k - 1
            ref = att_ref(p, coord)
            stages[p].append(send(ref, ref, at_send.at[s], at_recv.at[s], peer(order[2], k)))
        s = p * GATHER_SEMS + 9
        ref = att_ref(p, coord)
        to_sibling[p].append(send(ref, ref, at_send.at[s], at_recv.at[s], sibling))
    for k in (1, 3, 2):
        for p, (at, n, order) in enumerate(PARTS):
            stages[p][k - 1].wait_recv()
            s = p * GATHER_SEMS + 9 + k
            ref = att_ref(p, shifted(order[2], -k))
            to_sibling[p].append(send(ref, ref, at_send.at[s], at_recv.at[s], sibling))
    loads[2].wait()
    for p, (at, n, order) in enumerate(PARTS):
        for copy in to_sibling[p]:
            copy.wait_recv()
        block = jnp.concatenate([att[h].reshape(ROWS, HD) for h in range(at, at + n)], axis=1)
        delta = dot(wout[:, at * HD:(at + n) * HD], block, 1, 1)
        j = iota((ROWS, ROWS), 0)
        rest = sorted(order[:2], key=AXES.index)
        digits = {order[2]: lax.div(j, 32), rest[0]: lax.rem(lax.div(j, 4), 4), rest[1]: lax.rem(j, 4)}
        slot = ((digits["y"] * 4 + digits["z"]) * 4 + digits["x"]) * 2 + lax.rem(lax.div(j, 16), 2)
        to_seq = dot((slot == iota((ROWS, ROWS), 1)).astype(BF16), by_slot).astype(BF16)
        for _ in range(3):
            term = delta.astype(BF16)
            state = state + dot(term, to_seq)
            delta = delta - term.astype(F32)

    xf[own + (c,)] = (state * gain_f).astype(BF16)
    sf[own + (c,)] = jnp.sum(state * state, axis=0, keepdims=True)
    state_gather(xf, sf, xf_send, xf_recv, sf_send, sf_recv)
    loads[3].wait()
    loads[4].wait()
    for w, acc in ((wg, gate_ref), (wu, up_ref)):
        for y in range(4):
            block = xf[y].reshape(D // 4, ROWS)
            term = dot(w[:, y * (D // 4):(y + 1) * (D // 4)], block)
            acc[...] = term if y == 0 else acc[...] + term
    scale = row_scale(sf)
    gate = gate_ref[...] * scale
    hidden = gate / (1.0 + jnp.exp(-gate)) * (up_ref[...] * scale)
    hid_ref[...] = hidden.T.astype(BF16)

    loads[5].wait()
    half = ROWS // 2
    core_copies = []
    for y in range(4):
        def chunk(z, carry, y=y):
            lanes = pl.ds(pl.multiple_of((y * 4 + z) * 512, 512), 512)
            term = dot(hid_ref[...], wd[:, lanes]).astype(BF16)
            for x in range(4):
                block = term[:, x * 128:(x + 1) * 128]
                pt[y, z, x, 0] = block[:half]
                pt[y, z, x, 1] = block[half:]
            return carry

        lax.fori_loop(0, 4, chunk, 0)
        core_copies.append(send(pt.at[y, :, :, 1 - c], rc.at[y], rs_send.at[y], rs_recv.at[y], sibling))
    for y in range(4):
        core_copies[y].wait_recv()
        pt[y, :, :, c] = (pt[y, :, :, c].astype(F32) + rc[y].astype(F32)).astype(BF16)

    arrivals = [[] for _ in PARTS]

    def reduced(p, stage):
        at, n, order = PARTS[p]
        rows = (pl.ds(at, n),)
        land = (rb0, rb1, rb2)[stage - 1]
        value = pt[index(coord, order[stage:]) + (c,) + rows].astype(F32)
        for k, copy in enumerate(arrivals[p]):
            copy.wait_recv()
            value = value + land[(k,) + (slice(None),) * (3 - stage) + rows].astype(F32)
        return value

    for stage in range(3):
        for p, (at, n, order) in enumerate(PARTS):
            rows = (pl.ds(at, n),)
            if stage:
                pt[index(coord, order[stage:]) + (c,) + rows] = reduced(p, stage).astype(BF16)
            arrivals[p] = []
            land = (rb0, rb1, rb2)[stage]
            for k in (1, 2, 3):
                src = pt.at[index(shifted(order[stage], k), order[stage + 1:]) + (c,) + rows]
                dst = land.at[(k - 1,) + (slice(None),) * (2 - stage) + rows]
                s = 4 + p * 9 + stage * 3 + k - 1
                arrivals[p].append(send(src, dst, rs_send.at[s], rs_recv.at[s], peer(order[stage], k)))
    for p, (at, n, order) in enumerate(PARTS):
        fs[c, pl.ds(at, n)] = reduced(p, 3)
    s = 4 + 9 * len(PARTS)
    copy = send(fs.at[c], fs.at[c], rs_send.at[s], rs_recv.at[s], sibling)
    copy.wait_recv()
    summed = fs[...].reshape(ROWS, 2 * FEATURES)
    summed = jnp.where(c == 0, summed[:, :FEATURES], summed[:, FEATURES:])
    state = jnp.concatenate([state, jnp.zeros_like(state)], axis=0).T[:, :FEATURES]
    out_ref[...] = state + summed
    for copy in pending:
        copy.wait_send()


def per_device(
    hidden_state, gain_attn, gain_ffn, w_qkv, w_out, w_gate, w_up, w_down, kv_cache, lengths, row_order
):
    parts = len(PARTS)
    vmem = pltpu.VMEM
    dma = pltpu.SemaphoreType.DMA
    scratch = [
        vmem((QKV, D), BF16), vmem((FEATURES, D), BF16), vmem((FF, D), BF16), vmem((FF, D), BF16),
        vmem((FF, D), BF16), vmem((1, CACHE, 2 * KVH * HD), BF16), dma((6,)),
        vmem((4, 4, 4, 2, FEATURES, ROWS), BF16), vmem((4, 4, 4, 2, 1, ROWS), F32),
        vmem((4, 4, 4, 2, FEATURES, ROWS), BF16), vmem((4, 4, 4, 2, 1, ROWS), F32),
        vmem((4, 4, 4, QH, HD), BF16), vmem((16 * 32, HD), F32), vmem((QH, 8, 16, HD), BF16),
        vmem((16, 8, 1, HD), F32), vmem((8, 16, 1, HD), F32), vmem((16, 8, 1, HD), F32),
        vmem((4, 4, 4, 2, ROWS // 2, 128), BF16), vmem((4, 4, 4, ROWS // 2, 128), BF16),
        vmem((3, 4, 4, ROWS // 2, 128), BF16), vmem((3, 4, ROWS // 2, 128), BF16),
        vmem((3, ROWS // 2, 128), BF16), vmem((2, ROWS // 2, 128), F32),
        vmem((ROWS, FF), BF16), vmem((FF, ROWS), F32), vmem((FF, ROWS), F32),
    ]
    for count in (parts * GATHER_SEMS, GATHER_SEMS, parts * GATHER_SEMS, GATHER_SEMS,
                  parts * GATHER_SEMS, 22, 5 + 9 * parts):
        scratch += [dma((count,)), dma((count,))]
    in_vmem = pl.BlockSpec(memory_space=pltpu.VMEM)
    anywhere = pl.BlockSpec(memory_space=pl.ANY)
    return pl.pallas_call(
        kernel,
        out_shape=jax.ShapeDtypeStruct((ROWS, FEATURES), F32),
        in_specs=[in_vmem] * 5 + [anywhere] * 6,
        out_specs=in_vmem,
        scratch_shapes=scratch,
        compiler_params=pltpu.CompilerParams(
            collective_id=0, has_side_effects=True, vmem_limit_bytes=56 * 1024 * 1024
        ),
    )(
        hidden_state, gain_attn.reshape(1, FEATURES), gain_ffn.reshape(1, FEATURES),
        lengths.reshape(1, ROWS), row_order.reshape(1, ROWS),
        w_qkv, w_out, w_gate, w_up, w_down, kv_cache,
    )


def solution(mesh):
    both = ("role", "grp")
    in_specs = (
        P(None, both), P(both), P(both), P(both, None), P(both, None), P(both, None),
        P(both, None), P(both, None), P(both, None, None), P(), P(),
    )
    return jax.shard_map(
        per_device, mesh=mesh, in_specs=in_specs, out_specs=P(None, both), check_vma=False
    )
```

```python
import jax
import jax.numpy as jnp
from jax import lax
from jax.experimental import pallas as pl
from jax.experimental.pallas import tpu as pltpu
from jax.sharding import PartitionSpec as P

F32 = jnp.float32
BF16 = jnp.bfloat16
D = 8192
QH = 64
KVH = 4
HD = 128
ROWS = 128
DEVICES = 128
FOLD = QH + 8
FEATURES = D // DEVICES
QKV = (QH + 2 * KVH) * HD // DEVICES
FF = 53248 // DEVICES
CACHE = 1024
EPS = 1e-05
AXES = "yzx"
MESH = pl.DeviceIdType.MESH

PARTS = ((0, 16, "x"), (16, 16, "z"), (32, 32, "y"))
OFFSETS = sorted(((i, j) for i in range(4) for j in range(4) if i or j),
                 key=lambda o: -sum(min(k, 4 - k) for k in o))


def iota(shape, dim):
    return lax.broadcasted_iota(jnp.int32, shape, dim)


def dot(a, b, ca=1, cb=0):
    return lax.dot_general(a, b, (((ca,), (cb,)), ((), ())), preferred_element_type=F32)


def kernel(
    hs_hbm, ga_ref, gf_ref, len_ref, ord_ref,
    wqkv_hbm, wout_hbm, wg_hbm, wu_hbm, wd_hbm, kv_hbm,
    out_ref,
    wqkv, wout, wg, wu, wd, kv, load_sem,
    hs, xa, sa, xf, sf, xt, f0, f1, f2, f3, att, t_buf, r1, r2,
    pt, rc, rb0, rb1, fs,
    hid_ref, gate_ref, up_ref,
    xa_send, xa_recv, sa_send, sa_recv, xf_send, xf_recv, sf_send, sf_recv,
    xt_send, xt_recv, aa_send, aa_recv, rs_send, rs_recv,
):
    role = lax.axis_index("role")
    grp = lax.axis_index("grp")
    c = lax.rem(grp, 2)
    coord = {
        "x": lax.rem(lax.div(grp, 2), 4),
        "z": lax.rem(lax.div(grp, 8), 4),
        "y": lax.div(grp, 32) * 2 + role,
    }
    me = role * 64 + grp

    def place_of(axis, value):
        return lax.rem(value, 2) * 2 + lax.div(value, 2) if axis == "y" else value

    def device(at, core):
        y = at["y"]
        return (lax.rem(y, 2), lax.div(y, 2) * 32 + at["z"] * 8 + at["x"] * 2 + core)

    def shifted(axis, k):
        return moved((axis,), (k,))

    def peer(axis, k):
        return device(shifted(axis, k), c)

    sibling = device(coord, 1 - c)

    def index(at, full=""):
        return tuple(slice(None) if a in full else place_of(a, at[a]) for a in AXES)

    def plane_of(axis):
        return AXES.replace(axis, "")

    def moved(axes, offsets):
        return {**coord, **{a: lax.rem(coord[a] + k + 4, 4) for a, k in zip(axes, offsets)}}

    def wait(ref, sem):
        pltpu.make_async_copy(ref, ref, sem).wait()

    pending = []

    def send(src, dst, send_sem, recv_sem, target):
        copy = pltpu.make_async_remote_copy(
            src_ref=src, dst_ref=dst, send_sem=send_sem, recv_sem=recv_sem,
            device_id=target, device_id_type=MESH,
        )
        copy.start()
        pending.append(copy)
        return copy

    loads = []
    for i, (src, dst) in enumerate(
        ((hs_hbm, hs), (wqkv_hbm, wqkv), (kv_hbm, kv), (wout_hbm, wout), (wg_hbm, wg), (wu_hbm, wu), (wd_hbm, wd))
    ):
        load = pltpu.make_async_copy(src, dst, load_sem.at[i])
        load.start()
        loads.append(load)

    others = [sibling]
    for axis in AXES:
        others += [device(moved(plane_of(axis), o), c) for o in OFFSETS if 0 not in o]
        others += [peer(axis, k) for k in (1, 2, 3)]
    for k in (1, 2, 3):
        others.append(device(shifted("x", k), 1 - c))
    barrier = pltpu.get_barrier_semaphore()
    for other in others:
        pl.semaphore_signal(barrier, inc=1, device_id=other, device_id_type=MESH)

    def transposed(v):
        return jnp.concatenate([v, jnp.zeros_like(v)], axis=1).T[:FEATURES]

    gain_f = transposed(jnp.broadcast_to(gf_ref[...], (ROWS, FEATURES)))
    gain_a = transposed(jnp.broadcast_to(ga_ref[...], (ROWS, FEATURES)))
    own = index(coord)
    loads[0].wait()
    state = transposed(hs[...])
    xa[own + (c,)] = (state * gain_a).astype(BF16)
    sa[own + (c,)] = jnp.sum(state * state, axis=0, keepdims=True)

    order_row = ord_ref[...]
    by_seq = (iota((ROWS, ROWS), 0) == order_row).astype(F32)
    by_slot = by_seq.T.astype(BF16)
    lane = iota((1, ROWS), 1)
    my_seq = jnp.sum(jnp.where(lane == me, order_row, 0), axis=1, keepdims=True)
    my_len = jnp.sum(jnp.where(lane == my_seq, len_ref[...], 0), axis=1, keepdims=True)

    pl.semaphore_wait(barrier, len(others))

    class Gather:
        def __init__(self, buf, axis, tail, send_sem, recv_sem, base):
            self.buf, self.axis, self.tail = buf, axis, tail
            self.plane = plane_of(axis)
            self.send_sem, self.recv_sem, self.base = send_sem.at[base], recv_sem, base * 12

        def at(self, where):
            return self.buf.at[where + (c,) + self.tail]

        def sem(self, stage, row):
            return self.recv_sem.at[self.base + stage * 4 + row]

        def row(self, k):
            return index(moved(self.plane[:1], (k,)), self.plane[1:])

        def push(self, ref, sem, target):
            pltpu.make_async_remote_copy(
                src_ref=ref, dst_ref=ref, send_sem=self.send_sem, recv_sem=sem,
                device_id=target, device_id_type=MESH,
            ).start()

        def spread(self, offset):
            sem = self.sem(0, (4 - offset[0]) % 4)
            self.push(self.at(own), sem, device(moved(self.plane, offset), c))

        def forward(self, k):
            where = self.row(k)
            some = tuple(pl.ds(0, 3) if a == self.plane[1] and k == 0 else w for a, w in zip(AXES, where))
            wait(self.at(some), self.sem(0, k))
            for j in (2, 1, 3):
                self.push(self.at(where), self.sem(1, k), peer(self.axis, j))

        def share(self, k):
            where = self.row(k)
            wait(self.at(tuple(pl.ds(0, 3) if a == self.axis else w for a, w in zip(AXES, where))), self.sem(1, k))
            where = tuple(slice(None) if a == self.axis else w for a, w in zip(AXES, where))
            self.push(self.at(where), self.sem(2, k), sibling)

        def finish(self, k):
            where = tuple(slice(None) if a == self.axis else w for a, w in zip(AXES, self.row(k)))
            wait(self.buf.at[where + (1 - c,) + self.tail], self.sem(2, k))

        def sent(self):
            blocks = self.buf.reshape(DEVICES, *self.buf.shape[4:])
            wait(blocks.at[(pl.ds(0, 127),) + self.tail], self.send_sem)

    gathered = []

    def gather(x, x_send, x_recv, s=None, s_send=None, s_recv=None):
        runs = [] if s is None else [Gather(s, "x", (), s_send, s_recv, 0)]
        for p, (at, n, axis) in enumerate(PARTS):
            runs.append(Gather(x, axis, (pl.ds(at, n),), x_send, x_recv, p))
        for offset in OFFSETS:
            for run in runs:
                run.spread(offset)
        for step in ("forward", "share", "finish"):
            for k in (0, 1, 3, 2):
                for run in runs:
                    getattr(run, step)(k)
        gathered.extend(runs)

    def row_scale(s):
        total = jnp.sum(s[...].reshape(DEVICES, ROWS), axis=0, keepdims=True)
        return lax.rsqrt(total * (1.0 / D) + EPS)

    gather(xa, xa_send, xa_recv, sa, sa_send, sa_recv)
    loads[1].wait()
    proj = jnp.zeros((QKV, ROWS), F32)
    for y in range(4):
        block = xa[y].reshape(D // 4, ROWS)
        proj = proj + dot(wqkv[:, y * (D // 4):(y + 1) * (D // 4)], block)
    proj = (proj * row_scale(sa)).astype(BF16)

    lane_of = lax.rem(me * QKV + iota((QKV, HD), 0), HD)
    place = (lane_of == iota((QKV, HD), 1)).astype(BF16)
    placed = dot(proj, place, 0, 0).astype(BF16)
    t_buf[...] = dot(by_slot, placed).reshape(16, 8, 1, HD)
    xc = coord["x"] * 2 + c
    yz = place_of("y", coord["y"]) * 4 + coord["z"]
    first, second = [], []
    n = 0
    for kx in range(4):
        for kc in range(2):
            if kx or kc:
                at, core = shifted("x", kx), lax.rem(c + kc, 2)
                first.append(send(t_buf.at[:, at["x"] * 2 + core], r1.at[xc],
                                  aa_send.at[n], aa_recv.at[n], device(at, core)))
                n += 1
    r1[xc] = t_buf[:, xc]
    for copy in first:
        copy.wait_recv()
    for o in OFFSETS:
        at = moved("yz", o)
        second.append(send(r1.at[:, place_of("y", at["y"]) * 4 + at["z"]], r2.at[yz],
                           aa_send.at[n], aa_recv.at[n], device(at, c)))
        n += 1
    r2[yz] = r1[:, yz]
    for copy in second:
        copy.wait_recv()
    got = r2[...].reshape(DEVICES, HD)
    start = iota((DEVICES, HD), 0) * QKV
    late = iota((DEVICES, HD), 1) >= lax.rem(start, HD)
    heads = QH + 2 * KVH
    src_head = lax.div(iota((heads, DEVICES), 1) * QKV, HD)
    head = iota((heads, DEVICES), 0)
    qkv = dot((src_head == head).astype(BF16), jnp.where(late, got, 0.0).astype(BF16))
    qkv = qkv + dot((src_head + 1 == head).astype(BF16), jnp.where(late, 0.0, got).astype(BF16))

    loads[2].wait()
    groups = QH // KVH
    valid = iota((groups, CACHE), 1) < my_len
    outs = []
    for h in range(KVH):
        q = qkv[h * groups:(h + 1) * groups]
        k_new = qkv[QH + h:QH + h + 1]
        v_new = qkv[QH + KVH + h:QH + KVH + h + 1]
        keys = kv[0, :, h * HD:(h + 1) * HD]
        values = kv[0, :, (KVH + h) * HD:(KVH + h + 1) * HD]
        cached = jnp.where(valid, dot(q.astype(BF16), keys, 1, 1) * (1.0 / HD ** 0.5), -1e30)
        fresh = jnp.sum(q * k_new, axis=1, keepdims=True) * (1.0 / HD ** 0.5)
        top = jnp.maximum(jnp.max(cached, axis=1, keepdims=True), fresh)
        cached_w = jnp.where(valid, jnp.exp(cached - top), 0.0)
        fresh_w = jnp.exp(fresh - top)
        total = jnp.sum(cached_w, axis=1, keepdims=True) + fresh_w
        summed = dot(cached_w.astype(BF16), values) + fresh_w.astype(BF16).astype(F32) * v_new
        outs.append((summed / total).astype(BF16))
    xt[own + (c,)] = jnp.concatenate(outs, axis=0)

    gather(xt, xt_send, xt_recv)
    loads[3].wait()
    for y, fold in enumerate((f0, f1, f2, f3)):
        slots = ROWS // 4
        for i in range(slots):
            fold[i * FOLD:i * FOLD + QH] = xt[y, i // 8, i // 2 % 4, i % 2].astype(F32)
        for h in range(QH):
            att[h, y * slots:(y + 1) * slots] = fold[pl.ds(h, slots, stride=FOLD)].astype(BF16)
    delta = jnp.zeros((FEATURES, ROWS), F32)
    for h in range(0, QH, 16):
        block = jnp.concatenate([att[i] for i in range(h, h + 16)], axis=1)
        delta = delta + dot(wout[:, h * HD:(h + 16) * HD], block, 1, 1)
    for _ in range(3):
        term = delta.astype(BF16)
        state = state + dot(term, by_slot)
        delta = delta - term.astype(F32)

    xf[own + (c,)] = (state * gain_f).astype(BF16)
    sf[own + (c,)] = jnp.sum(state * state, axis=0, keepdims=True)
    gather(xf, xf_send, xf_recv, sf, sf_send, sf_recv)
    loads[4].wait()
    loads[5].wait()
    for w, acc in ((wg, gate_ref), (wu, up_ref)):
        for y in range(4):
            block = xf[y].reshape(D // 4, ROWS)
            term = dot(w[:, y * (D // 4):(y + 1) * (D // 4)], block)
            acc[...] = term if y == 0 else acc[...] + term
    scale = row_scale(sf)
    gate = gate_ref[...] * scale
    hidden = gate / (1.0 + jnp.exp(-gate)) * (up_ref[...] * scale)
    hid_ref[...] = hidden.T.astype(BF16)

    loads[6].wait()
    half = ROWS // 2
    slabs = (2, 1, 3, 0)
    lines = (slice(None),) * 2

    def push(src, dst, send_sem, recv_sem, target):
        pltpu.make_async_remote_copy(
            src_ref=src, dst_ref=dst, send_sem=send_sem, recv_sem=recv_sem,
            device_id=target, device_id_type=MESH,
        ).start()

    def slab_of(k):
        return place_of("y", moved("y", (k,))["y"])

    def down(k):
        y = slab_of(k)

        def chunk(z, carry):
            lanes = pl.ds(pl.multiple_of((y * 4 + z) * 512, 512), 512)
            term = dot(hid_ref[...], wd[:, lanes]).astype(BF16)
            for x in range(4):
                block = term[:, x * 128:(x + 1) * 128]
                pt[y, z, x, 0] = block[:half]
                pt[y, z, x, 1] = block[half:]
            return carry

        lax.fori_loop(0, 4, chunk, 0)
        push(pt.at[y, :, :, 1 - c], rc.at[y], rs_send.at[0], rs_recv.at[k], sibling)

    def along(k):
        y = slab_of(k)
        wait(rc.at[y], rs_recv.at[k])
        pt[y, :, :, c] = (pt[y, :, :, c].astype(F32) + rc[y].astype(F32)).astype(BF16)
        for p, (at, n, axis) in enumerate(PARTS):
            rows = pl.ds(at, n)
            if axis == "y":
                if k:
                    push(pt.at[y, :, :, c, rows], rb0.at[k - 1, :, :, rows],
                         rs_send.at[1 + p], rs_recv.at[4 + p * 5], peer("y", k))
                continue
            for j in (2, 1, 3):
                where = index({**shifted(axis, j), "y": moved("y", (k,))["y"]}, plane_of(axis)[1:])
                push(pt.at[where + (c, rows)], rb0.at[j - 1, y, :, rows],
                     rs_send.at[1 + p], rs_recv.at[4 + p * 5 + k], peer(axis, j))

    def across(p, line, where, sem, offsets):
        at, n, axis = PARTS[p]
        rows = pl.ds(at, n)
        wait(rb0.at[(slice(None),) + line + (rows,)], rs_recv.at[sem])
        value = pt[where + (c, rows)].astype(F32)
        for j in range(3):
            value = value + rb0[(j,) + line + (rows,)].astype(F32)
        pt[where + (c, rows)] = value.astype(BF16)
        for o in offsets:
            target = moved(plane_of(axis), o)
            push(pt.at[index(target) + (c, rows)], rb1.at[o[0] * 4 + o[1], rows],
                 rs_send.at[1 + p], rs_recv.at[4 + p * 5 + 4], device(target, c))

    down(slabs[0])
    for i, k in enumerate(slabs):
        if i < 3:
            down(slabs[i + 1])
        along(k)
    for k in slabs:
        for p, (at, n, axis) in enumerate(PARTS):
            if axis == "y":
                if k == 0:
                    across(p, lines, index(coord, plane_of("y")), 4 + p * 5, OFFSETS)
            else:
                where = index(moved("y", (k,)), plane_of(axis)[1:])
                across(p, (slab_of(k), slice(None)), where, 4 + p * 5 + k,
                       [o for o in OFFSETS if o[0] == k])
    for p, (at, n, axis) in enumerate(PARTS):
        rows = pl.ds(at, n)
        wait(rb1.at[pl.ds(1, 15), rows], rs_recv.at[4 + p * 5 + 4])
        value = pt[own + (c, rows)].astype(F32)
        for i in range(1, 16):
            value = value + rb1[i, rows].astype(F32)
        fs[c, rows] = value
    push(fs.at[c], fs.at[c], rs_send.at[4], rs_recv.at[19], sibling)
    wait(fs.at[1 - c], rs_recv.at[19])
    summed = fs[...].reshape(ROWS, 2 * FEATURES)
    summed = jnp.where(c == 0, summed[:, :FEATURES], summed[:, FEATURES:])
    state = jnp.concatenate([state, jnp.zeros_like(state)], axis=0).T[:, :FEATURES]
    out_ref[...] = state + summed
    for copy in pending:
        copy.wait_send()
    for run in gathered:
        run.sent()
    wait(rc, rs_send.at[0])
    for p, (at, n, axis) in enumerate(PARTS):
        wait(rb0.at[:, :, :, pl.ds(at, n)], rs_send.at[1 + p])
        wait(rb1.at[pl.ds(1, 15), pl.ds(at, n)], rs_send.at[1 + p])
    wait(fs.at[c], rs_send.at[4])


def per_device(
    hidden_state, gain_attn, gain_ffn, w_qkv, w_out, w_gate, w_up, w_down, kv_cache, lengths, row_order
):
    parts = len(PARTS)
    vmem = pltpu.VMEM
    dma = pltpu.SemaphoreType.DMA
    scratch = [
        vmem((QKV, D), BF16), vmem((FEATURES, D), BF16), vmem((FF, D), BF16), vmem((FF, D), BF16),
        vmem((FF, D), BF16), vmem((1, CACHE, 2 * KVH * HD), BF16), dma((7,)), vmem((ROWS, FEATURES), F32),
        vmem((4, 4, 4, 2, FEATURES, ROWS), BF16), vmem((4, 4, 4, 2, 1, ROWS), F32),
        vmem((4, 4, 4, 2, FEATURES, ROWS), BF16), vmem((4, 4, 4, 2, 1, ROWS), F32),
        vmem((4, 4, 4, 2, QH, HD), BF16),
        *[vmem((ROWS // 4 * FOLD, HD), F32)] * 4, vmem((QH, ROWS, HD), BF16),
        vmem((16, 8, 1, HD), F32), vmem((8, 16, 1, HD), F32), vmem((16, 8, 1, HD), F32),
        vmem((4, 4, 4, 2, ROWS // 2, 128), BF16), vmem((4, 4, 4, ROWS // 2, 128), BF16),
        vmem((3, 4, 4, ROWS // 2, 128), BF16), vmem((16, ROWS // 2, 128), BF16),
        vmem((2, ROWS // 2, 128), F32),
        vmem((ROWS, FF), BF16), vmem((FF, ROWS), F32), vmem((FF, ROWS), F32),
    ]
    for send_count, count in ((parts, parts * 12), (1, 12), (parts, parts * 12), (1, 12), (parts, parts * 12),
                              (22, 22), (5, 20)):
        scratch += [dma((send_count,)), dma((count,))]
    in_vmem = pl.BlockSpec(memory_space=pltpu.VMEM)
    anywhere = pl.BlockSpec(memory_space=pl.ANY)
    return pl.pallas_call(
        kernel,
        out_shape=jax.ShapeDtypeStruct((ROWS, FEATURES), F32),
        in_specs=[anywhere] + [in_vmem] * 4 + [anywhere] * 6,
        out_specs=in_vmem,
        scratch_shapes=scratch,
        compiler_params=pltpu.CompilerParams(
            collective_id=0, has_side_effects=True, vmem_limit_bytes=56 * 1024 * 1024
        ),
    )(
        hidden_state, gain_attn.reshape(1, FEATURES), gain_ffn.reshape(1, FEATURES),
        lengths.reshape(1, ROWS), row_order.reshape(1, ROWS),
        w_qkv, w_out, w_gate, w_up, w_down, kv_cache,
    )


def solution(mesh):
    both = ("role", "grp")
    in_specs = (
        P(None, both), P(both), P(both), P(both, None), P(both, None), P(both, None),
        P(both, None), P(both, None), P(both, None, None), P(), P(),
    )
    return jax.shard_map(
        per_device, mesh=mesh, in_specs=in_specs, out_specs=P(None, both), check_vma=False
    )
```

```python
import jax
import jax.numpy as jnp
from jax import lax
from jax.experimental import pallas as pl
from jax.experimental.pallas import tpu as pltpu
from jax.sharding import PartitionSpec as P

F32 = jnp.float32
BF16 = jnp.bfloat16
D = 8192
QH = 64
KVH = 4
HD = 128
ROWS = 128
DEVICES = 128
FOLD = QH + 8
FEATURES = D // DEVICES
QKV = (QH + 2 * KVH) * HD // DEVICES
FF = 53248 // DEVICES
CACHE = 1024
EPS = 1e-05
AXES = "yab"
MESH = pl.DeviceIdType.MESH

PARTS = ((0, 32, "b"), (32, 16, "a"), (48, 16, "y"))
GATHER_SEMS = 15
OFFSETS = sorted(((i, j) for i in range(4) for j in range(4) if i or j),
                 key=lambda o: -sum(min(k, 4 - k) for k in o))


def iota(shape, dim):
    return lax.broadcasted_iota(jnp.int32, shape, dim)


def dot(a, b, ca=1, cb=0):
    return lax.dot_general(a, b, (((ca,), (cb,)), ((), ())), preferred_element_type=F32)


def kernel(
    hs_hbm, ga_hbm, gf_hbm, len_hbm, ord_hbm,
    wqkv_hbm, wout_hbm, wg_hbm, wu_hbm, wd_hbm, kv_hbm,
    out_ref,
    wqkv, wout, wg, wu, wd, kv, load_sem,
    ga_ref, gf_ref, len_ref, ord_ref,
    hs, xa, sa, xf, sf, xt, f0, f1, att, t_buf, r1, r2,
    pt, rc, rb0, rb1, fs,
    hid_ref, gate_ref, up_ref,
    xa_send, xa_recv, sa_send, sa_recv, xf_send, xf_recv, sf_send, sf_recv,
    xt_send, xt_recv, aa_send, aa_recv, rs_send, rs_recv,
):
    role = lax.axis_index("role")
    grp = lax.axis_index("grp")
    c = lax.rem(grp, 2)
    here = {
        "x": lax.rem(lax.div(grp, 2), 4),
        "z": lax.rem(lax.div(grp, 8), 4),
        "y": lax.div(grp, 32) * 2 + role,
    }
    first_core = c == 0
    coord = {
        "y": here["y"],
        "a": jnp.where(first_core, here["z"], here["x"]),
        "b": jnp.where(first_core, here["x"], here["z"]),
    }
    me = role * 64 + grp

    def place_of(axis, value):
        return lax.rem(value, 2) * 2 + lax.div(value, 2) if axis == "y" else value

    def chip(x, y, z, core):
        return (lax.rem(y, 2), lax.div(y, 2) * 32 + z * 8 + x * 2 + core)

    def device(at):
        x = jnp.where(first_core, at["b"], at["a"])
        z = jnp.where(first_core, at["a"], at["b"])
        return chip(x, at["y"], z, c)

    def turned(value, k):
        return lax.rem(value + k + 4, 4)

    def shifted(axis, k):
        return moved((axis,), (k,))

    def peer(axis, k):
        return device(shifted(axis, k))

    sibling = chip(here["x"], here["y"], here["z"], 1 - c)

    def index(at, full=""):
        return tuple(slice(None) if a in full else place_of(a, at[a]) for a in AXES)

    def plane_of(axis):
        return AXES.replace(axis, "")

    def moved(axes, offsets):
        return {**coord, **{a: turned(coord[a], k) for a, k in zip(axes, offsets)}}

    def wait(ref, sem):
        pltpu.make_async_copy(ref, ref, sem).wait()

    pending = []

    def send(src, dst, send_sem, recv_sem, target):
        copy = pltpu.make_async_remote_copy(
            src_ref=src, dst_ref=dst, send_sem=send_sem, recv_sem=recv_sem,
            device_id=target, device_id_type=MESH,
        )
        copy.start()
        pending.append(copy)
        return copy

    loads = []
    for i, (src, dst) in enumerate(
        ((hs_hbm, hs), (ga_hbm, ga_ref), (gf_hbm, gf_ref), (len_hbm, len_ref), (ord_hbm, ord_ref), (wqkv_hbm, wqkv),
         (kv_hbm, kv), (wout_hbm, wout), (wg_hbm, wg), (wu_hbm, wu), (wd_hbm, wd))
    ):
        load = pltpu.make_async_copy(src, dst, load_sem.at[i])
        load.start()
        loads.append(load)

    others = [sibling]
    for axis in AXES:
        others += [device(moved(plane_of(axis), o)) for o in OFFSETS if 0 not in o]
        others += [peer(axis, k) for k in (1, 2, 3)]
    for k in (1, 2, 3):
        others.append(chip(turned(here["x"], k), here["y"], here["z"], 1 - c))
    barrier = pltpu.get_barrier_semaphore()
    for other in others:
        pl.semaphore_signal(barrier, inc=1, device_id=other, device_id_type=MESH)

    def gain_column(ref):
        gain = jnp.broadcast_to(ref[...], (ROWS, FEATURES))
        return jnp.concatenate([gain, gain], axis=1).T[:FEATURES]

    own = index(coord)
    loads[0].wait()
    loads[1].wait()
    gain_a = gain_column(ga_ref)
    state = hs[...]
    xa[own + (c,)] = (state * gain_a).astype(BF16)
    sa[0] = jnp.sum(state * state, axis=0, keepdims=True)
    pl.semaphore_wait(barrier, len(others))

    class Gather:
        def __init__(self, buf, axis, tail, send_sem, recv_sem, base):
            self.buf, self.axis, self.tail = buf, axis, tail
            self.plane = plane_of(axis)
            self.send_sem, self.recv_sem, self.base = send_sem.at[base], recv_sem, base * GATHER_SEMS

        def at(self, where):
            return self.buf.at[where + (c,) + self.tail]

        def sem(self, stage, row):
            return self.recv_sem.at[self.base + stage * 4 + row]

        def row(self, k):
            return index(moved(self.plane[:1], (k,)), self.plane[1:])

        def push(self, ref, sem, target):
            pltpu.make_async_remote_copy(
                src_ref=ref, dst_ref=ref, send_sem=self.send_sem, recv_sem=sem,
                device_id=target, device_id_type=MESH,
            ).start()

        def spread(self, offset):
            sem = self.sem(0, (4 - offset[0]) % 4) if offset[0] else self.sem(3, offset[1] - 1)
            self.push(self.at(own), sem, device(moved(self.plane, offset)))

        def along(self, where, k):
            for j in (2, 1, 3):
                self.push(self.at(where), self.sem(1, j if self.axis == "y" else k), peer(self.axis, j))

        def forward_near(self, j):
            where = index(moved(self.plane, (0, -j)))
            wait(self.at(where), self.sem(3, j - 1))
            self.along(where, 0)

        def forward(self, k):
            where = self.row(k)
            wait(self.at(where), self.sem(0, k))
            self.along(where, k)

        def share(self, k):
            slab = index(moved("y", (k,)), "ab")
            if self.axis != "y":
                some = tuple(pl.ds(0, 3) if a == self.axis else w for a, w in zip(AXES, slab))
                wait(self.at(some), self.sem(1, k))
            elif k:
                wait(self.at(slab), self.sem(1, 4 - k))
            self.push(self.at(slab), self.sem(2, k), sibling)

        def finish(self, k):
            wait(self.buf.at[index(moved("y", (k,)), "ab") + (1 - c,) + self.tail], self.sem(2, k))

        def sent(self):
            blocks = self.buf.reshape(DEVICES, *self.buf.shape[4:])
            wait(blocks.at[(pl.ds(0, 127),) + self.tail], self.send_sem)

    gathered = []

    class Squares:
        def __init__(self, buf, send_sem, recv_sem):
            self.buf, self.send_sem, self.recv_sem = buf, send_sem, recv_sem

        def push(self, row, to, sem, target):
            pltpu.make_async_remote_copy(
                src_ref=self.buf.at[row], dst_ref=self.buf.at[to], send_sem=self.send_sem.at[0],
                recv_sem=self.recv_sem.at[sem], device_id=target, device_id_type=MESH,
            ).start()

        def start(self):
            self.push(0, 4, 0, sibling)

        def step(self, stage):
            if stage == 0:
                wait(self.buf.at[4], self.recv_sem.at[0])
                self.buf[1] = self.buf[0] + self.buf[4]
            else:
                total = self.added(stage)
                self.buf[stage + 1] = total
            for k in (2, 1, 3):
                self.push(stage + 1, 5 + stage * 3 + k - 1, stage + 1, peer("bay"[stage], k))

        def added(self, stage):
            first = 5 + (stage - 1) * 3
            wait(self.buf.at[pl.ds(first, 3)], self.recv_sem.at[stage])
            return self.buf[stage] + self.buf[first] + self.buf[first + 1] + self.buf[first + 2]

        def scale(self):
            return lax.rsqrt(self.added(3) * (1.0 / D) + EPS)

        def sent(self):
            wait(self.buf.at[pl.ds(0, 10)], self.send_sem.at[0])

    def gather(x, x_send, x_recv, on_slab, squares=None, beside=None):
        runs = []
        for p, (at, n, axis) in enumerate(PARTS):
            runs.append(Gather(x, axis, (pl.ds(at, n),), x_send, x_recv, p))
        gathered.extend(runs)
        if squares is not None:
            gathered.append(squares)
            squares.start()
        for run in runs:
            run.along(own, 0)
        for offset in OFFSETS:
            for run in runs:
                run.spread(offset)
        if squares is not None:
            squares.step(0)
        if beside is not None:
            beside()
        for j in (1, 3, 2):
            for run in runs:
                run.forward_near(j)
        if squares is not None:
            squares.step(1)
        for k in (1, 3, 2):
            for run in runs:
                run.forward(k)
        if squares is not None:
            squares.step(2)
        order = (0, 1, 3, 2)
        for run in runs:
            run.share(0)
        for i, k in enumerate(order):
            for run in runs:
                if i < 3:
                    run.share(order[i + 1])
            for run in runs:
                run.finish(k)
            on_slab(i, place_of("y", moved("y", (k,))["y"]))

    def block_at(x, y, i):
        i, core = divmod(i, 2)
        return x[(y, i // 4, i % 4, 0) if core == 0 else (y, i % 4, i // 4, 1)]

    def slab_of_features(x, y):
        return jnp.concatenate([block_at(x, y, i) for i in range(ROWS // 4)], axis=0)

    def slab_lanes(y):
        return pl.ds(pl.multiple_of(y * (D // 4), D // 4), D // 4)

    first_squares = Squares(sa, sa_send, sa_recv)
    local = {}

    def one_hots():
        for load in loads[2:5]:
            load.wait()
        order_row = ord_ref[...]
        by_seq = (iota((ROWS, ROWS), 0) == order_row).astype(F32)
        local["by_slot"] = by_seq.T.astype(BF16)
        lane = iota((1, ROWS), 1)
        my_seq = jnp.sum(jnp.where(lane == me, order_row, 0), axis=1, keepdims=True)
        local["my_len"] = jnp.sum(jnp.where(lane == my_seq, len_ref[...], 0), axis=1, keepdims=True)
        local["gain_f"] = gain_column(gf_ref)
        loads[5].wait()

    def project(i, y):
        term = dot(wqkv[:, slab_lanes(y)], slab_of_features(xa, y))
        local["proj"] = local["proj"] + term if i else term

    gather(xa, xa_send, xa_recv, project, first_squares, one_hots)
    by_slot, my_len = local["by_slot"], local["my_len"]
    proj = (local["proj"] * first_squares.scale()).astype(BF16)

    lane_of = lax.rem(me * QKV + iota((QKV, HD), 0), HD)
    place = (lane_of == iota((QKV, HD), 1)).astype(BF16)
    placed = dot(proj, place, 0, 0).astype(BF16)
    t_buf[...] = dot(by_slot, placed).reshape(16, 8, 1, HD)
    xc = here["x"] * 2 + c
    yz = place_of("y", here["y"]) * 4 + here["z"]
    first, second = [], []
    n = 0
    for kx in (2, 1, 3, 0):
        for kc in (1, 0):
            if kx or kc:
                x, core = turned(here["x"], kx), lax.rem(c + kc, 2)
                first.append(send(t_buf.at[:, x * 2 + core], r1.at[xc], aa_send.at[n], aa_recv.at[n],
                                  chip(x, here["y"], here["z"], core)))
                n += 1
    r1[xc] = t_buf[:, xc]
    for copy in first:
        copy.wait_recv()
    for o in OFFSETS:
        y, z = turned(here["y"], o[0]), turned(here["z"], o[1])
        second.append(send(r1.at[:, place_of("y", y) * 4 + z], r2.at[yz], aa_send.at[n], aa_recv.at[n],
                           chip(here["x"], y, z, c)))
        n += 1
    r2[yz] = r1[:, yz]
    for copy in second:
        copy.wait_recv()
    got = r2[...].reshape(DEVICES, HD)
    start = iota((DEVICES, HD), 0) * QKV
    late = iota((DEVICES, HD), 1) >= lax.rem(start, HD)
    heads = QH + 2 * KVH
    src_head = lax.div(iota((heads, DEVICES), 1) * QKV, HD)
    head = iota((heads, DEVICES), 0)
    qkv = dot((src_head == head).astype(BF16), jnp.where(late, got, 0.0).astype(BF16))
    qkv = qkv + dot((src_head + 1 == head).astype(BF16), jnp.where(late, 0.0, got).astype(BF16))

    loads[6].wait()
    groups = QH // KVH
    valid = iota((groups, CACHE), 1) < my_len
    outs = []
    for h in range(KVH):
        q = qkv[h * groups:(h + 1) * groups]
        k_new = qkv[QH + h:QH + h + 1]
        v_new = qkv[QH + KVH + h:QH + KVH + h + 1]
        keys = kv[0, :, h * HD:(h + 1) * HD]
        values = kv[0, :, (KVH + h) * HD:(KVH + h + 1) * HD]
        cached = jnp.where(valid, dot(q.astype(BF16), keys, 1, 1) * (1.0 / HD ** 0.5), -1e30)
        fresh = jnp.sum(q * k_new, axis=1, keepdims=True) * (1.0 / HD ** 0.5)
        top = jnp.maximum(jnp.max(cached, axis=1, keepdims=True), fresh)
        cached_w = jnp.where(valid, jnp.exp(cached - top), 0.0)
        fresh_w = jnp.exp(fresh - top)
        total = jnp.sum(cached_w, axis=1, keepdims=True) + fresh_w
        summed = dot(cached_w.astype(BF16), values) + fresh_w.astype(BF16).astype(F32) * v_new
        outs.append((summed / total).astype(BF16))
    xt[own + (c,)] = jnp.concatenate(outs, axis=0)

    def regroup(i, y):
        fold = (f0, f1)[i % 2]
        slots = ROWS // 4
        for j in range(slots):
            fold[j * FOLD:j * FOLD + QH] = block_at(xt, y, j).astype(F32)
        rows = pl.ds(pl.multiple_of(y * slots, slots), slots)
        for h in range(QH):
            att[h, rows] = fold[pl.ds(h, slots, stride=FOLD)].astype(BF16)

    gather(xt, xt_send, xt_recv, regroup)
    loads[7].wait()
    delta = jnp.zeros((FEATURES, ROWS), F32)
    for h in range(0, QH, 16):
        block = jnp.concatenate([att[i] for i in range(h, h + 16)], axis=1)
        delta = delta + dot(wout[:, h * HD:(h + 16) * HD], block, 1, 1)
    for _ in range(3):
        term = delta.astype(BF16)
        state = state + dot(term, by_slot)
        delta = delta - term.astype(F32)

    xf[own + (c,)] = (state * local["gain_f"]).astype(BF16)
    sf[0] = jnp.sum(state * state, axis=0, keepdims=True)
    second_squares = Squares(sf, sf_send, sf_recv)

    def expand(i, y):
        block = slab_of_features(xf, y)
        for w, acc in ((wg, gate_ref), (wu, up_ref)):
            term = dot(w[:, slab_lanes(y)], block)
            acc[...] = acc[...] + term if i else term

    def weights():
        loads[8].wait()
        loads[9].wait()

    gather(xf, xf_send, xf_recv, expand, second_squares, weights)
    scale = second_squares.scale()
    gate = gate_ref[...] * scale
    hidden = gate / (1.0 + jnp.exp(-gate)) * (up_ref[...] * scale)
    hid_ref[...] = hidden.astype(BF16).T

    loads[10].wait()
    half = ROWS // 2
    slabs = (2, 1, 3, 0)

    def push(src, dst, send_sem, recv_sem, target):
        pltpu.make_async_remote_copy(
            src_ref=src, dst_ref=dst, send_sem=send_sem, recv_sem=recv_sem,
            device_id=target, device_id_type=MESH,
        ).start()

    def slab_of(k):
        return place_of("y", moved("y", (k,))["y"])

    def down(k):
        y = slab_of(k)

        def chunk(z, carry):
            lanes = pl.ds(pl.multiple_of((y * 4 + z) * 512, 512), 512)
            term = dot(hid_ref[...], wd[:, lanes]).astype(BF16)
            for x in range(4):
                block = term[:, x * 128:(x + 1) * 128]
                pt[y, z, x, 0] = block[:half]
                pt[y, x, z, 1] = block[half:]
            return carry

        lax.fori_loop(0, 4, chunk, 0)
        push(pt.at[y, :, :, 1 - c], rc.at[y], rs_send.at[0], rs_recv.at[k], sibling)

    def along(k):
        y = slab_of(k)
        wait(rc.at[y], rs_recv.at[k])
        pt[y, :, :, c] = (pt[y, :, :, c].astype(F32) + rc[y].astype(F32)).astype(BF16)
        for p, (at, n, axis) in enumerate(PARTS):
            rows = pl.ds(at, n)
            if axis == "y":
                if k:
                    push(pt.at[y, :, :, c, rows], rb0.at[k - 1, :, :, rows],
                         rs_send.at[1 + p], rs_recv.at[4 + p * 5], peer("y", k))
                continue
            for j in (2, 1, 3):
                where = index({**shifted(axis, j), "y": moved("y", (k,))["y"]}, plane_of(axis)[1:])
                push(pt.at[where + (c, rows)], rb0.at[j - 1, y, :, rows],
                     rs_send.at[1 + p], rs_recv.at[4 + p * 5 + k], peer(axis, j))

    def across(p, line, where, sem, offsets):
        at, n, axis = PARTS[p]
        rows = pl.ds(at, n)
        wait(rb0.at[(slice(None),) + line + (rows,)], rs_recv.at[sem])
        value = pt[where + (c, rows)].astype(F32)
        for j in range(3):
            value = value + rb0[(j,) + line + (rows,)].astype(F32)
        pt[where + (c, rows)] = value.astype(BF16)
        for o in offsets:
            target = moved(plane_of(axis), o)
            push(pt.at[index(target) + (c, rows)], rb1.at[o[0] * 4 + o[1], rows],
                 rs_send.at[1 + p], rs_recv.at[4 + p * 5 + 4], device(target))

    down(slabs[0])
    for i, k in enumerate(slabs):
        if i < 3:
            down(slabs[i + 1])
        along(k)
    for k in slabs:
        for p, (at, n, axis) in enumerate(PARTS):
            if axis != "y":
                where = index(moved("y", (k,)), plane_of(axis)[1:])
                across(p, (slab_of(k), slice(None)), where, 4 + p * 5 + k, [o for o in OFFSETS if o[0] == k])
            elif k == 1:
                across(p, (slice(None),) * 2, index(coord, "ab"), 4 + p * 5, OFFSETS)
    for p, (at, n, axis) in enumerate(PARTS):
        rows = pl.ds(at, n)
        wait(rb1.at[pl.ds(1, 15), rows], rs_recv.at[4 + p * 5 + 4])
        value = pt[own + (c, rows)].astype(F32)
        for i in range(1, 16):
            value = value + rb1[i, rows].astype(F32)
        fs[c, rows] = value
    push(fs.at[c], fs.at[c], rs_send.at[4], rs_recv.at[19], sibling)
    wait(fs.at[1 - c], rs_recv.at[19])
    summed = fs[...].reshape(ROWS, 2 * FEATURES)
    summed = jnp.where(c == 0, summed[:, :FEATURES], summed[:, FEATURES:])
    out_ref[...] = state + jnp.concatenate([summed, jnp.zeros_like(summed)], axis=1).T[:FEATURES]
    for copy in pending:
        copy.wait_send()
    for run in gathered:
        run.sent()
    wait(rc, rs_send.at[0])
    for p, (at, n, axis) in enumerate(PARTS):
        wait(rb0.at[:, :, :, pl.ds(at, n)], rs_send.at[1 + p])
        wait(rb1.at[pl.ds(1, 15), pl.ds(at, n)], rs_send.at[1 + p])
    wait(fs.at[c], rs_send.at[4])


def per_device(
    hidden_state, gain_attn, gain_ffn, w_qkv, w_out, w_gate, w_up, w_down, kv_cache, lengths, row_order
):
    parts = len(PARTS)
    vmem = pltpu.VMEM
    dma = pltpu.SemaphoreType.DMA
    scratch = [
        vmem((QKV, D), BF16), vmem((FEATURES, D), BF16), vmem((FF, D), BF16), vmem((FF, D), BF16),
        vmem((FF, D), BF16), vmem((1, CACHE, 2 * KVH * HD), BF16), dma((11,)),
        vmem((1, FEATURES), F32), vmem((1, FEATURES), F32), vmem((1, ROWS), jnp.int32), vmem((1, ROWS), jnp.int32),
        vmem((FEATURES, ROWS), F32),
        vmem((4, 4, 4, 2, FEATURES, ROWS), BF16), vmem((14, 1, ROWS), F32),
        vmem((4, 4, 4, 2, FEATURES, ROWS), BF16), vmem((14, 1, ROWS), F32),
        vmem((4, 4, 4, 2, QH, HD), BF16),
        *[vmem((ROWS // 4 * FOLD, HD), F32)] * 2, vmem((QH, ROWS, HD), BF16),
        vmem((16, 8, 1, HD), F32), vmem((8, 16, 1, HD), F32), vmem((16, 8, 1, HD), F32),
        vmem((4, 4, 4, 2, ROWS // 2, 128), BF16), vmem((4, 4, 4, ROWS // 2, 128), BF16),
        vmem((3, 4, 4, ROWS // 2, 128), BF16), vmem((16, ROWS // 2, 128), BF16),
        vmem((2, ROWS // 2, 128), F32),
        vmem((ROWS, FF), BF16), vmem((FF, ROWS), F32), vmem((FF, ROWS), F32),
    ]
    for send_count, count in ((parts, parts * GATHER_SEMS), (1, 4), (parts, parts * GATHER_SEMS), (1, 4),
                              (parts, parts * GATHER_SEMS), (22, 22), (5, 20)):
        scratch += [dma((send_count,)), dma((count,))]
    in_vmem = pl.BlockSpec(memory_space=pltpu.VMEM)
    anywhere = pl.BlockSpec(memory_space=pl.ANY)
    out = pl.pallas_call(
        kernel,
        out_shape=jax.ShapeDtypeStruct((FEATURES, ROWS), F32),
        in_specs=[anywhere] * 11,
        out_specs=in_vmem,
        scratch_shapes=scratch,
        compiler_params=pltpu.CompilerParams(
            collective_id=0, has_side_effects=True, vmem_limit_bytes=56 * 1024 * 1024
        ),
    )(
        hidden_state.T, gain_attn.reshape(1, FEATURES), gain_ffn.reshape(1, FEATURES),
        lengths.reshape(1, ROWS), row_order.reshape(1, ROWS),
        w_qkv, w_out, w_gate, w_up, w_down, kv_cache,
    )
    return out.T


def solution(mesh):
    both = ("role", "grp")
    in_specs = (
        P(None, both), P(both), P(both), P(both, None), P(both, None), P(both, None),
        P(both, None), P(both, None), P(both, None, None), P(), P(),
    )
    return jax.shard_map(
        per_device, mesh=mesh, in_specs=in_specs, out_specs=P(None, both), check_vma=False
    )
```

```python
import jax
import jax.numpy as jnp
from jax import lax
from jax.experimental import pallas as pl
from jax.experimental.pallas import tpu as pltpu
from jax.sharding import PartitionSpec as P

F32 = jnp.float32
BF16 = jnp.bfloat16
D = 8192
QH = 64
KVH = 4
HD = 128
ROWS = 128
DEVICES = 128
FOLD = QH + 8
FEATURES = D // DEVICES
QKV = (QH + 2 * KVH) * HD // DEVICES
FF = 53248 // DEVICES
CACHE = 1024
EPS = 1e-05
AXES = "yab"
MESH = pl.DeviceIdType.MESH

PARTS = ((0, 32, "b"), (32, 16, "a"), (48, 16, "y"))
GATHER_SEMS = 15


def hops(*offsets):
    return sum(min(k, 4 - k) for k in offsets)


OFFSETS = sorted(((i, j) for i in range(4) for j in range(4) if i or j), key=lambda o: -hops(*o))


def iota(shape, dim):
    return lax.broadcasted_iota(jnp.int32, shape, dim)


def dot(a, b, ca=1, cb=0):
    return lax.dot_general(a, b, (((ca,), (cb,)), ((), ())), preferred_element_type=F32)


def kernel(
    hs_hbm, ga_hbm, gf_hbm, len_hbm, ord_hbm,
    wqkv_hbm, wout_hbm, wg_hbm, wu_hbm, wd_hbm, kv_hbm,
    out_ref,
    wqkv, wout, wg, wu, wd, kv, load_sem,
    ga_ref, gf_ref, len_ref, ord_ref,
    hs, xa, sa, xf, sf, xt, f0, f1, att, t_buf, r1, r2,
    pt, rc, rb0, rb1,
    hid_ref, gate_ref, up_ref,
    xa_send, xa_recv, sa_send, sa_recv, xf_send, xf_recv, sf_send, sf_recv,
    xt_send, xt_recv, aa_send, aa_recv, rs_send, rs_recv,
):
    role = lax.axis_index("role")
    grp = lax.axis_index("grp")
    c = lax.rem(grp, 2)
    here = {
        "x": lax.rem(lax.div(grp, 2), 4),
        "z": lax.rem(lax.div(grp, 8), 4),
        "y": lax.div(grp, 32) * 2 + role,
    }
    first_core = c == 0
    coord = {
        "y": here["y"],
        "a": jnp.where(first_core, here["z"], here["x"]),
        "b": jnp.where(first_core, here["x"], here["z"]),
    }
    me = role * 64 + grp

    def place_of(axis, value):
        return lax.rem(value, 2) * 2 + lax.div(value, 2) if axis == "y" else value

    def chip(x, y, z, core):
        return (lax.rem(y, 2), lax.div(y, 2) * 32 + z * 8 + x * 2 + core)

    def device(at):
        x = jnp.where(first_core, at["b"], at["a"])
        z = jnp.where(first_core, at["a"], at["b"])
        return chip(x, at["y"], z, c)

    def turned(value, k):
        return lax.rem(value + k + 4, 4)

    def shifted(axis, k):
        return moved((axis,), (k,))

    def peer(axis, k):
        return device(shifted(axis, k))

    sibling = chip(here["x"], here["y"], here["z"], 1 - c)

    def index(at, full=""):
        return tuple(slice(None) if a in full else place_of(a, at[a]) for a in AXES)

    def plane_of(axis):
        return AXES.replace(axis, "")

    def moved(axes, offsets):
        return {**coord, **{a: turned(coord[a], k) for a, k in zip(axes, offsets)}}

    def wait(ref, sem):
        pltpu.make_async_copy(ref, ref, sem).wait()

    pending = []

    def send(src, dst, send_sem, recv_sem, target):
        copy = pltpu.make_async_remote_copy(
            src_ref=src, dst_ref=dst, send_sem=send_sem, recv_sem=recv_sem,
            device_id=target, device_id_type=MESH,
        )
        copy.start()
        pending.append(copy)
        return copy

    loads = []
    for i, (src, dst) in enumerate(
        ((hs_hbm, hs), (ga_hbm, ga_ref), (gf_hbm, gf_ref), (len_hbm, len_ref), (ord_hbm, ord_ref), (wqkv_hbm, wqkv),
         (kv_hbm, kv), (wout_hbm, wout), (wg_hbm, wg), (wu_hbm, wu), (wd_hbm, wd))
    ):
        load = pltpu.make_async_copy(src, dst, load_sem.at[i])
        load.start()
        loads.append(load)

    others = {}
    for axis in AXES:
        plane = plane_of(axis)
        for o in OFFSETS:
            if 0 not in o:
                others.setdefault(hops(*o), []).append(device(moved(plane, o)))
        for k in (1, 2, 3):
            others.setdefault(hops(k), []).append(peer(axis, k))
    for k in (1, 2, 3):
        others[hops(k)].append(chip(turned(here["x"], k), here["y"], here["z"], 1 - c))
    others = [other for far in sorted(others, reverse=True) for other in others[far]] + [sibling]
    barrier = pltpu.get_barrier_semaphore()
    for other in others:
        pl.semaphore_signal(barrier, inc=1, device_id=other, device_id_type=MESH)

    def gain_column(ref):
        gain = jnp.broadcast_to(ref[...], (ROWS, FEATURES))
        return jnp.concatenate([gain, gain], axis=1).T[:FEATURES]

    own = index(coord)
    loads[0].wait()
    loads[1].wait()
    gain_a = gain_column(ga_ref)
    state = hs[...]
    xa[own + (c,)] = (state * gain_a).astype(BF16)
    sa[0] = jnp.sum(state * state, axis=0, keepdims=True)
    pl.semaphore_wait(barrier, len(others))

    class Gather:
        def __init__(self, buf, axis, tail, send_sem, recv_sem, base):
            self.buf, self.axis, self.tail = buf, axis, tail
            self.plane = plane_of(axis)
            self.send_sem, self.recv_sem, self.base = send_sem.at[base], recv_sem, base * GATHER_SEMS

        def at(self, where):
            return self.buf.at[where + (c,) + self.tail]

        def sem(self, stage, row):
            return self.recv_sem.at[self.base + stage * 4 + row]

        def row(self, k):
            return index(moved(self.plane[:1], (k,)), self.plane[1:])

        def push(self, ref, sem, target):
            pltpu.make_async_remote_copy(
                src_ref=ref, dst_ref=ref, send_sem=self.send_sem, recv_sem=sem,
                device_id=target, device_id_type=MESH,
            ).start()

        def spread(self, offset):
            sem = self.sem(0, (4 - offset[0]) % 4)
            self.push(self.at(own), sem, device(moved(self.plane, offset)))

        def along(self, where, k):
            for j in (2, 1, 3):
                self.push(self.at(where), self.sem(1, j if self.axis == "y" else k), peer(self.axis, j))

        def forward(self, k):
            where = self.row(k)
            come = where if k else tuple(pl.ds(0, 3) if a == self.plane[1] else w for a, w in zip(AXES, where))
            wait(self.at(come), self.sem(0, k))
            self.along(where, k)

        def share(self, k):
            slab = index(moved("y", (k,)), "ab")
            if self.axis != "y":
                some = tuple(pl.ds(0, 3) if a == self.axis else w for a, w in zip(AXES, slab))
                wait(self.at(some), self.sem(1, k))
            elif k:
                wait(self.at(slab), self.sem(1, 4 - k))
            self.push(self.at(slab), self.sem(2, k), sibling)

        def finish(self, k):
            wait(self.buf.at[index(moved("y", (k,)), "ab") + (1 - c,) + self.tail], self.sem(2, k))

        def sent(self):
            blocks = self.buf.reshape(DEVICES, *self.buf.shape[4:])
            wait(blocks.at[(pl.ds(0, 127),) + self.tail], self.send_sem)

    gathered = []

    class Squares:
        def __init__(self, buf, send_sem, recv_sem):
            self.buf, self.send_sem, self.recv_sem = buf, send_sem, recv_sem

        def push(self, row, to, sem, target):
            pltpu.make_async_remote_copy(
                src_ref=self.buf.at[row], dst_ref=self.buf.at[to], send_sem=self.send_sem.at[0],
                recv_sem=self.recv_sem.at[sem], device_id=target, device_id_type=MESH,
            ).start()

        def added(self, first, count, sem):
            wait(self.buf.at[pl.ds(first + 1, count)], self.recv_sem.at[sem])
            return jnp.sum(self.buf[first:first + count + 1].reshape(count + 1, ROWS), axis=0, keepdims=True)

        def spread(self, o):
            self.push(0, o[0] * 4 + o[1], 0, device(moved("ya", o)))

        def along(self):
            self.buf[17] = self.added(0, 15, 0)
            for k in (2, 1, 3):
                self.push(17, 17 + k, 1, peer("b", k))

        def share(self):
            self.buf[21] = self.added(17, 3, 1)
            self.push(21, 22, 2, sibling)

        def scale(self):
            return lax.rsqrt(self.added(21, 1, 2) * (1.0 / D) + EPS)

        def sent(self):
            wait(self.buf.at[pl.ds(0, 19)], self.send_sem.at[0])

    def gather(x, x_send, x_recv, on_slab, squares=None, beside=None, make=None):
        runs = []
        for p, (at, n, axis) in enumerate(PARTS):
            runs.append(Gather(x, axis, (pl.ds(at, n),), x_send, x_recv, p))
        gathered.extend(runs)
        if squares is not None:
            gathered.append(squares)
        if make is not None:
            for run, (at, n, axis) in zip(runs, PARTS):
                make(at, n)
                for offset in OFFSETS:
                    run.spread(offset)
        else:
            for offset in OFFSETS:
                for run in runs:
                    run.spread(offset)
                if squares is not None:
                    squares.spread(offset)
        if beside is not None:
            beside()
        for run in runs:
            run.forward(0)
        for k in (1, 3):
            for run in runs:
                run.forward(k)
        if squares is not None:
            squares.along()
        for run in runs:
            run.forward(2)
        order = (0, 1, 3, 2)
        for k in order[:3]:
            for run in runs:
                run.share(k)
        for i, k in enumerate(order):
            if squares is not None and i == 0:
                squares.share()
            for run in runs:
                run.finish(k)
            on_slab(i, place_of("y", moved("y", (k,))["y"]))
            if i == 0:
                for run in runs:
                    run.share(2)

    def block_at(x, y, i):
        i, core = divmod(i, 2)
        return x[(y, i // 4, i % 4, 0) if core == 0 else (y, i % 4, i // 4, 1)]

    def slab_of_features(x, y):
        return jnp.concatenate([block_at(x, y, i) for i in range(ROWS // 4)], axis=0)

    def slab_lanes(y):
        return pl.ds(pl.multiple_of(y * (D // 4), D // 4), D // 4)

    first_squares = Squares(sa, sa_send, sa_recv)
    local = {}

    def one_hots():
        for load in loads[2:5]:
            load.wait()
        order_row = ord_ref[...]
        by_seq = (iota((ROWS, ROWS), 0) == order_row).astype(F32)
        local["by_slot"] = by_seq.T.astype(BF16)
        lane = iota((1, ROWS), 1)
        my_seq = jnp.sum(jnp.where(lane == me, order_row, 0), axis=1, keepdims=True)
        local["my_len"] = jnp.sum(jnp.where(lane == my_seq, len_ref[...], 0), axis=1, keepdims=True)
        local["gain_f"] = gain_column(gf_ref)
        loads[5].wait()

    def project(i, y):
        term = dot(wqkv[:, slab_lanes(y)], slab_of_features(xa, y))
        local["proj"] = local["proj"] + term if i else term

    gather(xa, xa_send, xa_recv, project, first_squares, one_hots)
    by_slot, my_len = local["by_slot"], local["my_len"]
    proj = (local["proj"] * first_squares.scale()).astype(BF16)

    lane_of = lax.rem(me * QKV + iota((QKV, HD), 0), HD)
    place = (lane_of == iota((QKV, HD), 1)).astype(BF16)
    placed = dot(proj, place, 0, 0).astype(BF16)
    t_buf[...] = dot(by_slot, placed).reshape(16, 8, 1, HD)
    xc = here["x"] * 2 + c
    yz = place_of("y", here["y"]) * 4 + here["z"]
    first, second = [], []
    n = 0
    for kx in (2, 1, 3, 0):
        for kc in (1, 0):
            if kx or kc:
                x, core = turned(here["x"], kx), lax.rem(c + kc, 2)
                first.append(send(t_buf.at[:, x * 2 + core], r1.at[xc], aa_send.at[n], aa_recv.at[n],
                                  chip(x, here["y"], here["z"], core)))
                n += 1
    r1[xc] = t_buf[:, xc]
    for copy in first:
        copy.wait_recv()
    for o in OFFSETS:
        y, z = turned(here["y"], o[0]), turned(here["z"], o[1])
        second.append(send(r1.at[:, place_of("y", y) * 4 + z], r2.at[yz], aa_send.at[n], aa_recv.at[n],
                           chip(here["x"], y, z, c)))
        n += 1
    r2[yz] = r1[:, yz]
    for copy in second:
        copy.wait_recv()
    got = r2[...].reshape(DEVICES, HD)
    start = iota((DEVICES, HD), 0) * QKV
    late = iota((DEVICES, HD), 1) >= lax.rem(start, HD)
    heads = QH + 2 * KVH
    src_head = lax.div(iota((heads, DEVICES), 1) * QKV, HD)
    head = iota((heads, DEVICES), 0)
    qkv = dot((src_head == head).astype(BF16), jnp.where(late, got, 0.0).astype(BF16))
    qkv = qkv + dot((src_head + 1 == head).astype(BF16), jnp.where(late, 0.0, got).astype(BF16))

    loads[6].wait()
    groups = QH // KVH
    valid = iota((groups, CACHE), 1) < my_len

    def attend(h):
        q = qkv[h * groups:(h + 1) * groups]
        k_new = qkv[QH + h:QH + h + 1]
        v_new = qkv[QH + KVH + h:QH + KVH + h + 1]
        keys = kv[0, :, h * HD:(h + 1) * HD]
        values = kv[0, :, (KVH + h) * HD:(KVH + h + 1) * HD]
        cached = jnp.where(valid, dot(q.astype(BF16), keys, 1, 1) * (1.0 / HD ** 0.5), -1e30)
        fresh = jnp.sum(q * k_new, axis=1, keepdims=True) * (1.0 / HD ** 0.5)
        top = jnp.maximum(jnp.max(cached, axis=1, keepdims=True), fresh)
        cached_w = jnp.where(valid, jnp.exp(cached - top), 0.0)
        fresh_w = jnp.exp(fresh - top)
        total = jnp.sum(cached_w, axis=1, keepdims=True) + fresh_w
        summed = dot(cached_w.astype(BF16), values) + fresh_w.astype(BF16).astype(F32) * v_new
        xt[own + (c, slice(h * groups, (h + 1) * groups))] = (summed / total).astype(BF16)

    def regroup(i, y):
        fold = (f0, f1)[i % 2]
        slots = ROWS // 4
        for j in range(slots):
            fold[j * FOLD:j * FOLD + QH] = block_at(xt, y, j).astype(F32)
        rows = pl.ds(pl.multiple_of(y * slots, slots), slots)
        for h in range(QH):
            att[h, rows] = fold[pl.ds(h, slots, stride=FOLD)].astype(BF16)

    def attend_rows(at, n):
        for h in range(at // groups, (at + n) // groups):
            attend(h)

    gather(xt, xt_send, xt_recv, regroup, make=attend_rows)
    loads[7].wait()
    delta = jnp.zeros((FEATURES, ROWS), F32)
    for h in range(0, QH, 16):
        block = jnp.concatenate([att[i] for i in range(h, h + 16)], axis=1)
        delta = delta + dot(wout[:, h * HD:(h + 16) * HD], block, 1, 1)
    for _ in range(2):
        term = delta.astype(BF16)
        state = state + dot(term, by_slot)
        delta = delta - term.astype(F32)

    xf[own + (c,)] = (state * local["gain_f"]).astype(BF16)
    sf[0] = jnp.sum(state * state, axis=0, keepdims=True)
    second_squares = Squares(sf, sf_send, sf_recv)

    def expand(i, y):
        block = slab_of_features(xf, y)
        for w, acc in ((wg, gate_ref), (wu, up_ref)):
            term = dot(w[:, slab_lanes(y)], block)
            acc[...] = acc[...] + term if i else term

    def weights():
        loads[8].wait()
        loads[9].wait()

    gather(xf, xf_send, xf_recv, expand, second_squares, weights)
    scale = second_squares.scale()
    gate = gate_ref[...] * scale
    hidden = gate / (1.0 + jnp.exp(-gate)) * (up_ref[...] * scale)
    hid_ref[...] = hidden.astype(BF16)

    loads[10].wait()
    slabs = (2, 1, 3, 0)

    def push(src, dst, send_sem, recv_sem, target):
        pltpu.make_async_remote_copy(
            src_ref=src, dst_ref=dst, send_sem=send_sem, recv_sem=recv_sem,
            device_id=target, device_id_type=MESH,
        ).start()

    def slab_of(k):
        return place_of("y", moved("y", (k,))["y"])

    def down(k):
        y = slab_of(k)

        term = dot(wd[:, slab_lanes(y)], hid_ref[...], 0, 0).astype(BF16)
        for z in range(4):
            for x in range(4):
                block = term[(z * 4 + x) * 128:(z * 4 + x + 1) * 128]
                pt[y, z, x, 0] = block[:FEATURES]
                pt[y, x, z, 1] = block[FEATURES:]
        push(pt.at[y, :, :, 1 - c], rc.at[y], rs_send.at[0], rs_recv.at[k], sibling)

    def along(k):
        y = slab_of(k)
        wait(rc.at[y], rs_recv.at[k])
        pt[y, :, :, c] = (pt[y, :, :, c].astype(F32) + rc[y].astype(F32)).astype(BF16)
        for p, (at, n, axis) in enumerate(PARTS):
            rows = pl.ds(at, n)
            if axis == "y":
                if k:
                    push(pt.at[y, :, :, c, rows], rb0.at[k - 1, :, :, rows],
                         rs_send.at[1 + p], rs_recv.at[4 + p * 5], peer("y", k))
                continue
            for j in (2, 1, 3):
                where = index({**shifted(axis, j), "y": moved("y", (k,))["y"]}, plane_of(axis)[1:])
                push(pt.at[where + (c, rows)], rb0.at[j - 1, y, :, rows],
                     rs_send.at[1 + p], rs_recv.at[4 + p * 5 + k], peer(axis, j))

    def across(p, line, where, sem, offsets):
        at, n, axis = PARTS[p]
        rows = pl.ds(at, n)
        wait(rb0.at[(slice(None),) + line + (rows,)], rs_recv.at[sem])
        value = pt[where + (c, rows)].astype(F32)
        for j in range(3):
            value = value + rb0[(j,) + line + (rows,)].astype(F32)
        pt[where + (c, rows)] = value.astype(BF16)
        for o in offsets:
            target = moved(plane_of(axis), o)
            push(pt.at[index(target) + (c, rows)], rb1.at[o[0] * 4 + o[1], rows],
                 rs_send.at[1 + p], rs_recv.at[4 + p * 5 + 4], device(target))

    down(slabs[0])
    for i, k in enumerate(slabs):
        if i < 3:
            down(slabs[i + 1])
        along(k)
    for k in slabs:
        for p, (at, n, axis) in enumerate(PARTS):
            if axis != "y":
                where = index(moved("y", (k,)), plane_of(axis)[1:])
                across(p, (slab_of(k), slice(None)), where, 4 + p * 5 + k, [o for o in OFFSETS if o[0] == k])
            elif k == 1:
                across(p, (slice(None),) * 2, index(coord, "ab"), 4 + p * 5, OFFSETS)
    for p, (at, n, axis) in enumerate(PARTS):
        rows = pl.ds(at, n)
        wait(rb1.at[pl.ds(1, 15), rows], rs_recv.at[4 + p * 5 + 4])
        value = pt[own + (c, rows)].astype(F32)
        for i in range(1, 16):
            value = value + rb1[i, rows].astype(F32)
        out_ref[rows] = state[at:at + n] + value
    for copy in pending:
        copy.wait_send()
    for run in gathered:
        run.sent()
    wait(rc, rs_send.at[0])
    for p, (at, n, axis) in enumerate(PARTS):
        wait(rb0.at[:, :, :, pl.ds(at, n)], rs_send.at[1 + p])
        wait(rb1.at[pl.ds(1, 15), pl.ds(at, n)], rs_send.at[1 + p])


def per_device(
    hidden_state, gain_attn, gain_ffn, w_qkv, w_out, w_gate, w_up, w_down, kv_cache, lengths, row_order
):
    parts = len(PARTS)
    vmem = pltpu.VMEM
    dma = pltpu.SemaphoreType.DMA
    scratch = [
        vmem((QKV, D), BF16), vmem((FEATURES, D), BF16), vmem((FF, D), BF16), vmem((FF, D), BF16),
        vmem((FF, D), BF16), vmem((1, CACHE, 2 * KVH * HD), BF16), dma((11,)),
        vmem((1, FEATURES), F32), vmem((1, FEATURES), F32), vmem((1, ROWS), jnp.int32), vmem((1, ROWS), jnp.int32),
        vmem((FEATURES, ROWS), F32),
        vmem((4, 4, 4, 2, FEATURES, ROWS), BF16), vmem((23, 1, ROWS), F32),
        vmem((4, 4, 4, 2, FEATURES, ROWS), BF16), vmem((23, 1, ROWS), F32),
        vmem((4, 4, 4, 2, QH, HD), BF16),
        *[vmem((ROWS // 4 * FOLD, HD), F32)] * 2, vmem((QH, ROWS, HD), BF16),
        vmem((16, 8, 1, HD), F32), vmem((8, 16, 1, HD), F32), vmem((16, 8, 1, HD), F32),
        vmem((4, 4, 4, 2, FEATURES, ROWS), BF16), vmem((4, 4, 4, FEATURES, ROWS), BF16),
        vmem((3, 4, 4, FEATURES, ROWS), BF16), vmem((16, FEATURES, ROWS), BF16),
        vmem((FF, ROWS), BF16), vmem((FF, ROWS), F32), vmem((FF, ROWS), F32),
    ]
    for send_count, count in ((parts, parts * GATHER_SEMS), (1, 4), (parts, parts * GATHER_SEMS), (1, 4),
                              (parts, parts * GATHER_SEMS), (22, 22), (4, 19)):
        scratch += [dma((send_count,)), dma((count,))]
    in_vmem = pl.BlockSpec(memory_space=pltpu.VMEM)
    anywhere = pl.BlockSpec(memory_space=pl.ANY)
    out = pl.pallas_call(
        kernel,
        out_shape=jax.ShapeDtypeStruct((FEATURES, ROWS), F32),
        in_specs=[anywhere] * 11,
        out_specs=in_vmem,
        scratch_shapes=scratch,
        compiler_params=pltpu.CompilerParams(
            collective_id=0, has_side_effects=True, vmem_limit_bytes=56 * 1024 * 1024
        ),
    )(
        hidden_state.T, gain_attn.reshape(1, FEATURES), gain_ffn.reshape(1, FEATURES),
        lengths.reshape(1, ROWS), row_order.reshape(1, ROWS),
        w_qkv, w_out, w_gate, w_up, w_down, kv_cache,
    )
    return out.T


def solution(mesh):
    both = ("role", "grp")
    in_specs = (
        P(None, both), P(both), P(both), P(both, None), P(both, None), P(both, None),
        P(both, None), P(both, None), P(both, None, None), P(), P(),
    )
    return jax.shard_map(
        per_device, mesh=mesh, in_specs=in_specs, out_specs=P(None, both), check_vma=False
    )
```

```python
import jax
import jax.numpy as jnp
from jax import lax
from jax.experimental import pallas as pl
from jax.experimental.pallas import tpu as pltpu
from jax.sharding import PartitionSpec as P

F32 = jnp.float32
BF16 = jnp.bfloat16
D = 8192
QH = 64
KVH = 4
HD = 128
ROWS = 128
DEVICES = 128
FOLD = QH + 8
FEATURES = D // DEVICES
QKV = (QH + 2 * KVH) * HD // DEVICES
FF = 53248 // DEVICES
CACHE = 1024
EPS = 1e-05
AXES = "yab"
MESH = pl.DeviceIdType.MESH

PARTS = ((0, 32, "b"), (32, 16, "a"), (48, 16, "y"))
GATHER_SEMS = 15


def hops(*offsets):
    return sum(min(k, 4 - k) for k in offsets)


OFFSETS = sorted(((i, j) for i in range(4) for j in range(4) if i or j), key=lambda o: -hops(*o))


def iota(shape, dim):
    return lax.broadcasted_iota(jnp.int32, shape, dim)


def dot(a, b, ca=1, cb=0):
    return lax.dot_general(a, b, (((ca,), (cb,)), ((), ())), preferred_element_type=F32)


def kernel(
    hs_hbm, ga_hbm, gf_hbm, len_hbm, ord_hbm,
    wqkv_hbm, wout_hbm, wg_hbm, wu_hbm, wd_hbm, kv_hbm,
    out_ref,
    wqkv, wout, wg, wu, wd, kv, load_sem,
    ga_ref, gf_ref, len_ref, ord_ref,
    hs, xa, sa, xf, sf, xt, f0, f1, att, t_buf, r1, r2,
    pt, rc, rb0, rb1,
    hid_ref, gate_ref, up_ref,
    xa_send, xa_recv, sa_send, sa_recv, xf_send, xf_recv, sf_send, sf_recv,
    xt_send, xt_recv, aa_send, aa_recv, rs_send, rs_recv,
):
    role = lax.axis_index("role")
    grp = lax.axis_index("grp")
    c = lax.rem(grp, 2)
    here = {
        "x": lax.rem(lax.div(grp, 2), 4),
        "z": lax.rem(lax.div(grp, 8), 4),
        "y": lax.div(grp, 32) * 2 + role,
    }
    first_core = c == 0
    coord = {
        "y": here["y"],
        "a": jnp.where(first_core, here["z"], here["x"]),
        "b": jnp.where(first_core, here["x"], here["z"]),
    }
    me = role * 64 + grp

    def place_of(axis, value):
        return lax.rem(value, 2) * 2 + lax.div(value, 2) if axis == "y" else value

    def chip(x, y, z, core):
        return (lax.rem(y, 2), lax.div(y, 2) * 32 + z * 8 + x * 2 + core)

    def device(at):
        x = jnp.where(first_core, at["b"], at["a"])
        z = jnp.where(first_core, at["a"], at["b"])
        return chip(x, at["y"], z, c)

    def turned(value, k):
        return lax.rem(value + k + 4, 4)

    def shifted(axis, k):
        return moved((axis,), (k,))

    def peer(axis, k):
        return device(shifted(axis, k))

    sibling = chip(here["x"], here["y"], here["z"], 1 - c)

    def index(at, full=""):
        return tuple(slice(None) if a in full else place_of(a, at[a]) for a in AXES)

    def plane_of(axis):
        return AXES.replace(axis, "")

    def moved(axes, offsets):
        return {**coord, **{a: turned(coord[a], k) for a, k in zip(axes, offsets)}}

    def wait(ref, sem):
        pltpu.make_async_copy(ref, ref, sem).wait()

    pending = []

    def send(src, dst, send_sem, recv_sem, target):
        copy = pltpu.make_async_remote_copy(
            src_ref=src, dst_ref=dst, send_sem=send_sem, recv_sem=recv_sem,
            device_id=target, device_id_type=MESH,
        )
        copy.start()
        pending.append(copy)
        return copy

    loads = []
    for i, (src, dst) in enumerate(
        ((hs_hbm, hs), (ga_hbm, ga_ref), (gf_hbm, gf_ref), (len_hbm, len_ref), (ord_hbm, ord_ref), (wqkv_hbm, wqkv),
         (kv_hbm, kv), (wout_hbm, wout), (wg_hbm, wg), (wu_hbm, wu), (wd_hbm, wd))
    ):
        load = pltpu.make_async_copy(src, dst, load_sem.at[i])
        load.start()
        loads.append(load)

    others = {}
    for axis in AXES:
        plane = plane_of(axis)
        for o in OFFSETS:
            if 0 not in o:
                others.setdefault(hops(*o), []).append(device(moved(plane, o)))
        for k in (1, 2, 3):
            others.setdefault(hops(k), []).append(peer(axis, k))
    for k in (1, 2, 3):
        others[hops(k)].append(chip(turned(here["x"], k), here["y"], here["z"], 1 - c))
    others = [other for far in sorted(others, reverse=True) for other in others[far]] + [sibling]
    barrier = pltpu.get_barrier_semaphore()
    for other in others:
        pl.semaphore_signal(barrier, inc=1, device_id=other, device_id_type=MESH)

    def gain_column(ref):
        gain = jnp.broadcast_to(ref[...], (ROWS, FEATURES))
        return jnp.concatenate([gain, gain], axis=1).T[:FEATURES]

    own = index(coord)
    loads[0].wait()
    loads[1].wait()
    gain_a = gain_column(ga_ref)
    state = hs[...]
    xa[own + (c,)] = (state * gain_a).astype(BF16)
    sa[0] = jnp.sum(state * state, axis=0, keepdims=True)
    pl.semaphore_wait(barrier, len(others))

    class Gather:
        def __init__(self, buf, axis, tail, send_sem, recv_sem, base):
            self.buf, self.axis, self.tail = buf, axis, tail
            self.plane = plane_of(axis)
            self.send_sem, self.recv_sem, self.base = send_sem.at[base], recv_sem, base * GATHER_SEMS

        def at(self, where):
            return self.buf.at[where + (c,) + self.tail]

        def sem(self, stage, row):
            return self.recv_sem.at[self.base + stage * 4 + row]

        def row(self, k):
            return index(moved(self.plane[:1], (k,)), self.plane[1:])

        def push(self, ref, sem, target):
            pltpu.make_async_remote_copy(
                src_ref=ref, dst_ref=ref, send_sem=self.send_sem, recv_sem=sem,
                device_id=target, device_id_type=MESH,
            ).start()

        def spread(self, offset):
            sem = self.sem(0, (4 - offset[0]) % 4)
            self.push(self.at(own), sem, device(moved(self.plane, offset)))

        def along(self, where, k):
            for j in (2, 1, 3):
                self.push(self.at(where), self.sem(1, j if self.axis == "y" else k), peer(self.axis, j))

        def forward(self, k):
            where = self.row(k)
            come = where if k else tuple(pl.ds(0, 3) if a == self.plane[1] else w for a, w in zip(AXES, where))
            wait(self.at(come), self.sem(0, k))
            self.along(where, k)

        def share(self, k):
            slab = index(moved("y", (k,)), "ab")
            if self.axis != "y":
                some = tuple(pl.ds(0, 3) if a == self.axis else w for a, w in zip(AXES, slab))
                wait(self.at(some), self.sem(1, k))
            elif k:
                wait(self.at(slab), self.sem(1, 4 - k))
            self.push(self.at(slab), self.sem(2, k), sibling)

        def finish(self, k):
            wait(self.buf.at[index(moved("y", (k,)), "ab") + (1 - c,) + self.tail], self.sem(2, k))

        def sent(self):
            blocks = self.buf.reshape(DEVICES, *self.buf.shape[4:])
            wait(blocks.at[(pl.ds(0, 127),) + self.tail], self.send_sem)

    gathered = []

    class Squares:
        def __init__(self, buf, send_sem, recv_sem):
            self.buf, self.send_sem, self.recv_sem = buf, send_sem, recv_sem

        def push(self, row, to, sem, target):
            pltpu.make_async_remote_copy(
                src_ref=self.buf.at[row], dst_ref=self.buf.at[to], send_sem=self.send_sem.at[0],
                recv_sem=self.recv_sem.at[sem], device_id=target, device_id_type=MESH,
            ).start()

        def added(self, first, count, sem):
            wait(self.buf.at[pl.ds(first + 1, count)], self.recv_sem.at[sem])
            return jnp.sum(self.buf[first:first + count + 1].reshape(count + 1, ROWS), axis=0, keepdims=True)

        def spread(self, o):
            self.push(0, o[0] * 4 + o[1], 0, device(moved("ya", o)))

        def along(self):
            self.buf[17] = self.added(0, 15, 0)
            for k in (2, 1, 3):
                self.push(17, 17 + k, 1, peer("b", k))

        def share(self):
            self.buf[21] = self.added(17, 3, 1)
            self.push(21, 22, 2, sibling)

        def scale(self):
            return lax.rsqrt(self.added(21, 1, 2) * (1.0 / D) + EPS)

        def sent(self):
            wait(self.buf.at[pl.ds(0, 19)], self.send_sem.at[0])

    def gather(x, x_send, x_recv, on_slab, squares=None, beside=None, make=None):
        runs = []
        for p, (at, n, axis) in enumerate(PARTS):
            runs.append(Gather(x, axis, (pl.ds(at, n),), x_send, x_recv, p))
        gathered.extend(runs)
        if squares is not None:
            gathered.append(squares)
        if make is not None:
            for run, (at, n, axis) in zip(runs, PARTS):
                make(at, n)
                for offset in OFFSETS:
                    run.spread(offset)
        else:
            for offset in OFFSETS:
                for run in runs:
                    run.spread(offset)
                if squares is not None:
                    squares.spread(offset)
        if beside is not None:
            beside()
        for run in runs:
            run.forward(0)
        for k in (1, 3):
            for run in runs:
                run.forward(k)
        if squares is not None:
            squares.along()
        for run in reversed(runs):
            run.forward(2)
        order = (0, 1, 3, 2)
        for k in order[:3]:
            for run in runs:
                run.share(k)
        for i, k in enumerate(order):
            if squares is not None and i == 0:
                squares.share()
            for run in runs:
                run.finish(k)
            on_slab(i, place_of("y", moved("y", (k,))["y"]))
            if i == 0:
                for run in runs:
                    run.share(2)

    def block_at(x, y, i):
        i, core = divmod(i, 2)
        return x[(y, i // 4, i % 4, 0) if core == 0 else (y, i % 4, i // 4, 1)]

    def slab_of_features(x, y):
        return jnp.concatenate([block_at(x, y, i) for i in range(ROWS // 4)], axis=0)

    def slab_lanes(y):
        return pl.ds(pl.multiple_of(y * (D // 4), D // 4), D // 4)

    first_squares = Squares(sa, sa_send, sa_recv)
    local = {}

    def one_hots():
        for load in loads[2:5]:
            load.wait()
        order_row = ord_ref[...]
        by_seq = (iota((ROWS, ROWS), 0) == order_row).astype(F32)
        local["by_slot"] = by_seq.T.astype(BF16)
        lane = iota((1, ROWS), 1)
        my_seq = jnp.sum(jnp.where(lane == me, order_row, 0), axis=1, keepdims=True)
        local["my_len"] = jnp.sum(jnp.where(lane == my_seq, len_ref[...], 0), axis=1, keepdims=True)
        local["gain_f"] = gain_column(gf_ref)
        loads[5].wait()

    def project(i, y):
        term = dot(wqkv[:, slab_lanes(y)], slab_of_features(xa, y))
        local["proj"] = local["proj"] + term if i else term

    gather(xa, xa_send, xa_recv, project, first_squares, one_hots)
    by_slot, my_len = local["by_slot"], local["my_len"]
    proj = (local["proj"] * first_squares.scale()).astype(BF16)

    lane_of = lax.rem(me * QKV + iota((QKV, HD), 0), HD)
    place = (lane_of == iota((QKV, HD), 1)).astype(BF16)
    placed = dot(proj, place, 0, 0).astype(BF16)
    t_buf[...] = dot(by_slot, placed).reshape(16, 8, 1, HD)
    xc = here["x"] * 2 + c
    yz = place_of("y", here["y"]) * 4 + here["z"]
    first, second = [], []
    n = 0
    for kx in (2, 1, 3, 0):
        for kc in (1, 0):
            if kx or kc:
                x, core = turned(here["x"], kx), lax.rem(c + kc, 2)
                first.append(send(t_buf.at[:, x * 2 + core], r1.at[xc], aa_send.at[n], aa_recv.at[n],
                                  chip(x, here["y"], here["z"], core)))
                n += 1
    r1[xc] = t_buf[:, xc]
    for copy in first:
        copy.wait_recv()
    for o in OFFSETS:
        y, z = turned(here["y"], o[0]), turned(here["z"], o[1])
        second.append(send(r1.at[:, place_of("y", y) * 4 + z], r2.at[yz], aa_send.at[n], aa_recv.at[n],
                           chip(here["x"], y, z, c)))
        n += 1
    r2[yz] = r1[:, yz]
    for copy in second:
        copy.wait_recv()
    got = r2[...].reshape(DEVICES, HD)
    start = iota((DEVICES, HD), 0) * QKV
    late = iota((DEVICES, HD), 1) >= lax.rem(start, HD)
    heads = QH + 2 * KVH
    src_head = lax.div(iota((heads, DEVICES), 1) * QKV, HD)
    head = iota((heads, DEVICES), 0)
    qkv = dot((src_head == head).astype(BF16), jnp.where(late, got, 0.0).astype(BF16))
    qkv = qkv + dot((src_head + 1 == head).astype(BF16), jnp.where(late, 0.0, got).astype(BF16))

    loads[6].wait()
    groups = QH // KVH
    valid = iota((groups, CACHE), 1) < my_len

    def attend(h):
        q = qkv[h * groups:(h + 1) * groups]
        k_new = qkv[QH + h:QH + h + 1]
        v_new = qkv[QH + KVH + h:QH + KVH + h + 1]
        keys = kv[0, :, h * HD:(h + 1) * HD]
        values = kv[0, :, (KVH + h) * HD:(KVH + h + 1) * HD]
        cached = jnp.where(valid, dot(q.astype(BF16), keys, 1, 1) * (1.0 / HD ** 0.5), -1e30)
        fresh = jnp.sum(q * k_new, axis=1, keepdims=True) * (1.0 / HD ** 0.5)
        top = jnp.maximum(jnp.max(cached, axis=1, keepdims=True), fresh)
        cached_w = jnp.where(valid, jnp.exp(cached - top), 0.0)
        fresh_w = jnp.exp(fresh - top)
        total = jnp.sum(cached_w, axis=1, keepdims=True) + fresh_w
        summed = dot(cached_w.astype(BF16), values) + fresh_w.astype(BF16).astype(F32) * v_new
        xt[own + (c, slice(h * groups, (h + 1) * groups))] = (summed / total).astype(BF16)

    def regroup(i, y):
        fold = (f0, f1)[i % 2]
        slots = ROWS // 4
        for j in range(slots):
            fold[j * FOLD:j * FOLD + QH] = block_at(xt, y, j).astype(F32)
        rows = pl.ds(pl.multiple_of(y * slots, slots), slots)
        for h in range(QH):
            att[h, rows] = fold[pl.ds(h, slots, stride=FOLD)].astype(BF16)

    def attend_rows(at, n):
        for h in range(at // groups, (at + n) // groups):
            attend(h)

    gather(xt, xt_send, xt_recv, regroup, make=attend_rows)
    loads[7].wait()
    delta = jnp.zeros((FEATURES, ROWS), F32)
    for h in range(0, QH, 16):
        block = jnp.concatenate([att[i] for i in range(h, h + 16)], axis=1)
        delta = delta + dot(wout[:, h * HD:(h + 16) * HD], block, 1, 1)
    for _ in range(2):
        term = delta.astype(BF16)
        state = state + dot(term, by_slot)
        delta = delta - term.astype(F32)

    xf[own + (c,)] = (state * local["gain_f"]).astype(BF16)
    sf[0] = jnp.sum(state * state, axis=0, keepdims=True)
    second_squares = Squares(sf, sf_send, sf_recv)

    def expand(i, y):
        block = slab_of_features(xf, y)
        for w, acc in ((wg, gate_ref), (wu, up_ref)):
            term = dot(w[:, slab_lanes(y)], block)
            acc[...] = acc[...] + term if i else term

    def weights():
        loads[8].wait()
        loads[9].wait()

    gather(xf, xf_send, xf_recv, expand, second_squares, weights)
    scale = second_squares.scale()
    gate = gate_ref[...] * scale
    hidden = gate / (1.0 + jnp.exp(-gate)) * (up_ref[...] * scale)
    hid_ref[...] = hidden.astype(BF16)

    loads[10].wait()
    slabs = (2, 1, 3, 0)

    def push(src, dst, send_sem, recv_sem, target):
        pltpu.make_async_remote_copy(
            src_ref=src, dst_ref=dst, send_sem=send_sem, recv_sem=recv_sem,
            device_id=target, device_id_type=MESH,
        ).start()

    def slab_of(k):
        return place_of("y", moved("y", (k,))["y"])

    def down(k):
        y = slab_of(k)

        term = dot(wd[:, slab_lanes(y)], hid_ref[...], 0, 0).astype(BF16)
        for z in range(4):
            for x in range(4):
                block = term[(z * 4 + x) * 128:(z * 4 + x + 1) * 128]
                pt[y, z, x, 0] = block[:FEATURES]
                pt[y, x, z, 1] = block[FEATURES:]
        push(pt.at[y, :, :, 1 - c], rc.at[y], rs_send.at[0], rs_recv.at[k], sibling)

    def along(k):
        y = slab_of(k)
        wait(rc.at[y], rs_recv.at[k])
        pt[y, :, :, c] = (pt[y, :, :, c].astype(F32) + rc[y].astype(F32)).astype(BF16)
        for p, (at, n, axis) in enumerate(PARTS):
            rows = pl.ds(at, n)
            if axis == "y":
                if k:
                    push(pt.at[y, :, :, c, rows], rb0.at[k - 1, :, :, rows],
                         rs_send.at[1 + p], rs_recv.at[4 + p * 5], peer("y", k))
                continue
            for j in (2, 1, 3):
                where = index({**shifted(axis, j), "y": moved("y", (k,))["y"]}, plane_of(axis)[1:])
                push(pt.at[where + (c, rows)], rb0.at[j - 1, y, :, rows],
                     rs_send.at[1 + p], rs_recv.at[4 + p * 5 + k], peer(axis, j))

    def across(p, line, where, sem, offsets):
        at, n, axis = PARTS[p]
        rows = pl.ds(at, n)
        wait(rb0.at[(slice(None),) + line + (rows,)], rs_recv.at[sem])
        value = pt[where + (c, rows)].astype(F32)
        for j in range(3):
            value = value + rb0[(j,) + line + (rows,)].astype(F32)
        pt[where + (c, rows)] = value.astype(BF16)
        for o in offsets:
            target = moved(plane_of(axis), o)
            push(pt.at[index(target) + (c, rows)], rb1.at[o[0] * 4 + o[1], rows],
                 rs_send.at[1 + p], rs_recv.at[4 + p * 5 + 4], device(target))

    down(slabs[0])
    for i, k in enumerate(slabs):
        if i < 3:
            down(slabs[i + 1])
        along(k)
    for k in slabs:
        for p, (at, n, axis) in enumerate(PARTS):
            if axis != "y":
                where = index(moved("y", (k,)), plane_of(axis)[1:])
                across(p, (slab_of(k), slice(None)), where, 4 + p * 5 + k, [o for o in OFFSETS if o[0] == k])
            elif k == 3:
                across(p, (slice(None),) * 2, index(coord, "ab"), 4 + p * 5, OFFSETS)
    for p, (at, n, axis) in enumerate(PARTS):
        rows = pl.ds(at, n)
        wait(rb1.at[pl.ds(1, 15), rows], rs_recv.at[4 + p * 5 + 4])
        value = pt[own + (c, rows)].astype(F32)
        for i in range(1, 16):
            value = value + rb1[i, rows].astype(F32)
        out_ref[rows] = state[at:at + n] + value
    for copy in pending:
        copy.wait_send()
    for run in gathered:
        run.sent()
    wait(rc, rs_send.at[0])
    for p, (at, n, axis) in enumerate(PARTS):
        wait(rb0.at[:, :, :, pl.ds(at, n)], rs_send.at[1 + p])
        wait(rb1.at[pl.ds(1, 15), pl.ds(at, n)], rs_send.at[1 + p])


def per_device(
    hidden_state, gain_attn, gain_ffn, w_qkv, w_out, w_gate, w_up, w_down, kv_cache, lengths, row_order
):
    parts = len(PARTS)
    vmem = pltpu.VMEM
    dma = pltpu.SemaphoreType.DMA
    scratch = [
        vmem((QKV, D), BF16), vmem((FEATURES, D), BF16), vmem((FF, D), BF16), vmem((FF, D), BF16),
        vmem((FF, D), BF16), vmem((1, CACHE, 2 * KVH * HD), BF16), dma((11,)),
        vmem((1, FEATURES), F32), vmem((1, FEATURES), F32), vmem((1, ROWS), jnp.int32), vmem((1, ROWS), jnp.int32),
        vmem((FEATURES, ROWS), F32),
        vmem((4, 4, 4, 2, FEATURES, ROWS), BF16), vmem((23, 1, ROWS), F32),
        vmem((4, 4, 4, 2, FEATURES, ROWS), BF16), vmem((23, 1, ROWS), F32),
        vmem((4, 4, 4, 2, QH, HD), BF16),
        *[vmem((ROWS // 4 * FOLD, HD), F32)] * 2, vmem((QH, ROWS, HD), BF16),
        vmem((16, 8, 1, HD), F32), vmem((8, 16, 1, HD), F32), vmem((16, 8, 1, HD), F32),
        vmem((4, 4, 4, 2, FEATURES, ROWS), BF16), vmem((4, 4, 4, FEATURES, ROWS), BF16),
        vmem((3, 4, 4, FEATURES, ROWS), BF16), vmem((16, FEATURES, ROWS), BF16),
        vmem((FF, ROWS), BF16), vmem((FF, ROWS), F32), vmem((FF, ROWS), F32),
    ]
    for send_count, count in ((parts, parts * GATHER_SEMS), (1, 4), (parts, parts * GATHER_SEMS), (1, 4),
                              (parts, parts * GATHER_SEMS), (22, 22), (4, 19)):
        scratch += [dma((send_count,)), dma((count,))]
    in_vmem = pl.BlockSpec(memory_space=pltpu.VMEM)
    anywhere = pl.BlockSpec(memory_space=pl.ANY)
    out = pl.pallas_call(
        kernel,
        out_shape=jax.ShapeDtypeStruct((FEATURES, ROWS), F32),
        in_specs=[anywhere] * 11,
        out_specs=in_vmem,
        scratch_shapes=scratch,
        compiler_params=pltpu.CompilerParams(
            collective_id=0, has_side_effects=True, vmem_limit_bytes=56 * 1024 * 1024
        ),
    )(
        hidden_state.T, gain_attn.reshape(1, FEATURES), gain_ffn.reshape(1, FEATURES),
        lengths.reshape(1, ROWS), row_order.reshape(1, ROWS),
        w_qkv, w_out, w_gate, w_up, w_down, kv_cache,
    )
    return out.T


def solution(mesh):
    both = ("role", "grp")
    in_specs = (
        P(None, both), P(both), P(both), P(both, None), P(both, None), P(both, None),
        P(both, None), P(both, None), P(both, None, None), P(), P(),
    )
    return jax.shard_map(
        per_device, mesh=mesh, in_specs=in_specs, out_specs=P(None, both), check_vma=False
    )
```
